256 devices in a mesh: arch: 2 (over core), dom: 128 (over z, y, x).
Axes of the slice: x: 4, y: 4, z: 8, core: 2. Of those that a mesh axis runs over, the one named last changes fastest.
Arguments:
- position: float32 [3, 8388608], P(None, ('arch', 'dom')), may hold values from -6 to 6
- particle_mass: float32 [8388608], P(('arch', 'dom')), may hold values from 0.5 to 2
- settling: float32 [8388608], P(('arch', 'dom')), may hold values from 0.05 to 1
- walk_noise: float32 [3, 3, 8388608], P(None, None, ('arch', 'dom')), may hold values from -6 to 6
- velocity: bfloat16 [4, 3, 256, 2048], P(None, None, ('arch', 'dom')), may hold values from -6 to 6
- diffusivity: bfloat16 [4, 256, 2048], P(None, ('arch', 'dom')), may hold values from 0.019897461 to 0.5
- block_tile: int32 [3, 256, 128], P(None, ('arch', 'dom')), may hold values from 0 to 255, as said below
- cell_index: int32 [3, 8388608], P(None, ('arch', 'dom')), may hold values from 0 to 2047
- bed_cell: int32 [3, 8388608], P(None, ('arch', 'dom')), may hold values from 0 to 511
- route_code: int32 [2, 256, 128], P(None, ('arch', 'dom')), may hold values from 0 to 127, each once within a row
Outputs:
- final_position: float32 [3, 8388608], P(None, ('arch', 'dom'))
- final_mass: float32 [8388608], P(('arch', 'dom'))
- bed_deposit: float32 [256, 512], P(('arch', 'dom'))
The draws below stay inside these ranges and needn't reach their ends.
Inputs may be any that keep to these rules, and one draw needn't show every extreme that they name: `block_tile`: in every step each block's tile belongs to the group of the block's dom index d: (tile) % 128 equals d. Within each group, tiles held at lower arch indices are used by more blocks than those at higher ones.
All inputs are finite; a program needn't handle non-finite values.
Results may differ from the reference program's by a relative error of at most 0.0003.
Values may be sent and summed in bfloat16 or wider, within the bound.
No kernel may reach another device: no remote copies, remote signals or barrier semaphores. Data moves between devices by JAX's collectives and lax.ppermute only.
A program may use at most 64 MiB of HBM per device.

```python
import math
import jax
import jax.numpy as jnp

BLOCK = 256
BLK_PEER = 1
STEPS = 3
TILE_ARCH = 1
CELLS = 2048
BEDC = 512
SLABS = 4
NB = 128
PART_DEV = 32768
PARTICLES = 8388608
NT = 256
N_ARCH = 2
N_DOM = 128
DEVICES = 256


def draw_block_tile(key, part):
    keyed = jax.random.fold_in(key, 7)
    key_one, key_two, key_three = jax.random.split(keyed, 3)
    shape = (STEPS, DEVICES, NB)
    owner_one = jax.random.randint(key_one, shape, 0, N_ARCH)
    owner_two = jax.random.randint(key_two, shape, 0, N_ARCH)
    owner = jnp.minimum(owner_one, owner_two)
    within = jax.random.randint(key_three, shape, 0, TILE_ARCH)
    dom_ids = (jnp.arange(DEVICES, dtype=jnp.int32) % N_DOM)[None, :, None]
    tiles = (owner * N_DOM + dom_ids) * TILE_ARCH + within
    tiles = tiles.at[0, DEVICES - 1, 0].set(NT - 1)
    tiles = tiles.at[0, 0, 0].set(0)
    return tiles.astype(jnp.int32)


def touch_ends(array, rng, least, largest):
    shape = array.shape
    index_at = [jax.random.randint(jax.random.fold_in(rng, axis), (), 0, shape[axis]) for axis in range(len(shape))]
    array = array.at[tuple(index_at)].set(least)
    longest = shape.index(max(shape))
    index_at[longest] = (index_at[longest] + 1) % shape[longest]
    return array.at[tuple(index_at)].set(largest)


def level_of(stream_key, dims, shards, smallest, largest):
    def one(axis_at, blocks):
        heights = jax.random.uniform(jax.random.fold_in(jax.random.fold_in(stream_key, 6), axis_at), (blocks,), jnp.float32, smallest / len(shards), largest / len(shards))
        return jnp.repeat(jnp.exp(heights), dims[axis_at] // blocks).reshape((-1,) + (1,) * (len(dims) - axis_at - 1))

    loudness = one(*shards[0])
    for cut in shards[1:]:
        loudness = loudness * one(*cut)
    return loudness


def normal_values(stream_key, dims, width, bound, cuts=(), kind=jnp.bfloat16):
    drawn = jax.random.normal(stream_key, dims, jnp.float32) * width
    if len(cuts) > 0:
        drawn = level_of(stream_key, dims, cuts, -0.22, 0.18) * drawn
    return jnp.clip(drawn, min=-bound, max=bound).astype(kind)


def setup_inputs(seed: int = 0) -> dict:
    keys = jax.random.split(jax.random.key(seed), 11)
    return {
        "position": normal_values(keys[0], (3, PARTICLES), 1.0, 6.0, ((1, 256),), jnp.float32),
        "particle_mass": jnp.clip(jnp.exp(math.log(2.0) - 1.3862944 * jax.random.uniform(keys[1], (PARTICLES,), jnp.float32) ** level_of(keys[1], (PARTICLES,), ((0, 256),), -0.2, 0.2)), 0.5, 2.0),
        "settling": jnp.clip(jnp.exp(math.log(1.0) - 2.9957323 * jax.random.uniform(keys[2], (PARTICLES,), jnp.float32) ** level_of(keys[2], (PARTICLES,), ((0, 256),), -0.2, 0.2)), 0.05, 1.0),
        "walk_noise": normal_values(keys[3], (STEPS, 3, PARTICLES), 1.0, 6.0, ((2, 256),), jnp.float32),
        "velocity": normal_values(keys[4], (SLABS, 3, NT, CELLS), 1.0, 6.0, ((2, 256),)),
        "diffusivity": jnp.clip(jnp.exp(math.log(0.5) - 3.224016 * jax.random.uniform(keys[5], (SLABS, NT, CELLS), jnp.float32) ** level_of(keys[5], (SLABS, NT, CELLS), ((1, 256),), -0.2, 0.2)), 0.019897461, 0.5).astype(jnp.bfloat16),
        "block_tile": draw_block_tile(jax.random.fold_in(keys[10], 71), 0),
        "cell_index": touch_ends(jax.random.randint(keys[7], (STEPS, PARTICLES), 0, CELLS), jax.random.fold_in(keys[7], 1), 0, CELLS - 1).astype(jnp.int32),
        "bed_cell": touch_ends(jax.random.randint(keys[8], (STEPS, PARTICLES), 0, BEDC), jax.random.fold_in(keys[8], 1), 0, BEDC - 1).astype(jnp.int32),
        "route_code": jax.vmap(lambda own: jax.random.permutation(own, NB))(jax.random.split(keys[9], (STEPS - 1) * DEVICES)).reshape((STEPS - 1, DEVICES, NB)).astype(jnp.int32),
    }


time_step = 0.5

def reference(position, particle_mass, settling, walk_noise, velocity, diffusivity, block_tile, cell_index, bed_cell, route_code):
    bed_total = jnp.zeros((NT * BEDC,), jnp.float32)
    places = position
    masses = particle_mass
    speeds = settling
    device_ids = jnp.arange(DEVICES, dtype=jnp.int32)
    arch_ids = device_ids // N_DOM
    dom_ids = device_ids % N_DOM
    for step in range(STEPS):
        tiles = jnp.repeat(block_tile[step].reshape(-1), BLOCK).astype(jnp.int32)
        cells = cell_index[step]
        first_vel = velocity[step][:, tiles, cells].astype(jnp.float32)
        second_vel = velocity[step + 1][:, tiles, cells].astype(jnp.float32)
        first_diff = diffusivity[step][tiles, cells].astype(jnp.float32)
        second_diff = diffusivity[step + 1][tiles, cells].astype(jnp.float32)
        drift = 0.5 * time_step * (first_vel + second_vel)
        drift = drift.at[2].add(-time_step * speeds)
        places = places + drift + jnp.sqrt(time_step * (first_diff + second_diff)) * walk_noise[step]
        deposit = masses * (1.0 - jnp.exp(-time_step * speeds))
        masses = masses - deposit
        bins = (tiles * BEDC + bed_cell[step]).astype(jnp.int32)
        bed_total = bed_total.at[bins].add(deposit)
        if step + 1 < STEPS:
            codes = route_code[step]
            peers = codes // BLK_PEER
            within = codes % BLK_PEER
            target = ((arch_ids[:, None] * N_DOM + peers) * NB + dom_ids[:, None] * BLK_PEER + within).reshape(-1).astype(jnp.int32)
            place_blocks = places.reshape(3, DEVICES * NB, BLOCK)
            places = jnp.zeros_like(place_blocks).at[:, target].set(place_blocks).reshape(3, -1)
            mass_blocks = masses.reshape(DEVICES * NB, BLOCK)
            masses = jnp.zeros_like(mass_blocks).at[target].set(mass_blocks).reshape(-1)
            speed_blocks = speeds.reshape(DEVICES * NB, BLOCK)
            speeds = jnp.zeros_like(speed_blocks).at[target].set(speed_blocks).reshape(-1)
    scale_factor = TILE_ARCH * BEDC / PART_DEV
    return (places, masses, (bed_total * scale_factor).reshape(NT, BEDC))
```

```python
import jax
import jax.numpy as jnp
from jax import lax
from jax.experimental import pallas as pl
from jax.experimental.pallas import tpu as pltpu
from jax.sharding import PartitionSpec as P

NB = 128
WIDTH = 256
PARTS = NB * WIDTH
CELLS = 2048
ROWS = CELLS // 128
BEDC = 512
TILES = 128
DT = 0.5
CHUNK = 32
GROUP = 8

POS_SCALE = 2.0**26
MASS_SCALE = 32767.0
FRAC_SCALE = 166000.0

VMEM = pltpu.VMEM
SMEM = pltpu.SMEM


def whole(space=VMEM):
    return pl.BlockSpec(memory_space=space)


def params():
    return pltpu.CompilerParams(vmem_limit_bytes=40 * 1024 * 1024)


def sublane():
    return lax.broadcasted_iota(jnp.int32, (8, 128), 0)


def fill_tables(tables, own_vel, peer_vel, own_dif, peer_dif, slot, step, arch):
    for vel, dif, tile in ((own_vel, own_dif, arch), (peer_vel, peer_dif, 1 - arch)):
        for c in range(4):
            v = (vel[c] if c < 3 else dif[...]).astype(jnp.float32)
            total = v[step : step + 1] + v[step + 1 : step + 2]
            value = 0.5 * DT * total if c < 3 else jnp.sqrt(DT * total)
            for r in range(ROWS):
                row = value[:, 128 * r : 128 * (r + 1)]
                tables[slot, tile, r, c : c + 1, :] = row
                tables[slot, tile, r, c + 4 : c + 5, :] = row


def halves(low, high, sub):
    return jnp.where(sub < 4, jnp.broadcast_to(low, (8, 128)), jnp.broadcast_to(high, (8, 128)))


def stack_halves(ref, lead, start):
    low = ref[lead + (slice(None), pl.ds(start, 128))]
    high = ref[lead + (slice(None), pl.ds(start + 128, 128))]
    gap = jnp.zeros((1, 128), jnp.float32)
    return jnp.concatenate([low, gap, high, gap], axis=0)


def advance(tables, slot, tile, index, noise, sub):
    lane = index & 127
    values = [
        jnp.take_along_axis(tables[slot, tile, r], lane, axis=1, mode="promise_in_bounds")
        for r in range(ROWS)
    ]
    bit = 128
    while len(values) > 1:
        odd = (index & bit) != 0
        values = [jnp.where(odd, b, a) for a, b in zip(values[0::2], values[1::2])]
        bit *= 2
    value = values[0]
    spread = jnp.where((sub & 3) == 3, value, 0.0)
    spread = spread + pltpu.roll(spread, 7, 0)
    spread = spread + pltpu.roll(spread, 6, 0)
    return value + spread * noise


def cells_of(cell_ref, step, start, sub):
    low = cell_ref[step : step + 1, pl.ds(start, 128)]
    high = cell_ref[step : step + 1, pl.ds(start + 128, 128)]
    return halves(low, high, sub)


def fraction(settling):
    return 1.0 - jnp.exp(-DT * settling)


def first_kernel(
    tile_ref, route_ref, own_vel, peer_vel, own_dif, peer_dif,
    pos_ref, mass_ref, settle_ref, noise_ref, cell_ref, out_ref, tables, code_ref,
):
    arch = lax.axis_index("arch")
    part = pl.program_id(0)

    @pl.when(part == 0)
    def _():
        fill_tables(tables, own_vel, peer_vel, own_dif, peer_dif, 0, 0, arch)

    mass_code = (mass_ref[...] * MASS_SCALE + 0.5).astype(jnp.int32)
    mass_code = jnp.clip(mass_code, 0, 65535) - 32768
    frac_code = (fraction(settle_ref[...]) * FRAC_SCALE + 0.5).astype(jnp.int32)
    frac_code = jnp.clip(frac_code, 0, 65535)
    code_ref[...] = mass_code * 65536 + frac_code
    sub = sublane()
    state_row = (sub & 3) == 3
    fall = jnp.where((sub & 3) == 2, -3.0 * DT, 0.0)

    def block(j, carry):
        start = pl.multiple_of(j * WIDTH, WIDTH)
        slot = part * CHUNK + j
        index = cells_of(cell_ref, 0, start, sub)
        noise = stack_halves(noise_ref, (0,), start)
        here = stack_halves(pos_ref, (), start)
        speed = halves(settle_ref[pl.ds(2 * j, 1), :], settle_ref[pl.ds(2 * j + 1, 1), :], sub)
        here = here + fall * speed
        here = here + advance(tables, 0, tile_ref[0, 0, slot] // TILES, index, noise, sub)
        state = halves(code_ref[pl.ds(2 * j, 1), :], code_ref[pl.ds(2 * j + 1, 1), :], sub)
        code = jnp.where(state_row, state, (here * POS_SCALE).astype(jnp.int32))
        out_ref[route_ref[0, 0, slot]] = code
        return carry

    lax.fori_loop(0, CHUNK, block, 0, unroll=GROUP)


def later_kernel(
    tile_ref, own_vel, peer_vel, own_dif, peer_dif, noise_ref, cell_ref,
    second_ref, third_ref, tables,
):
    arch = lax.axis_index("arch")
    part = pl.program_id(0)

    @pl.when(part == 0)
    def _():
        for step in (1, 2):
            fill_tables(tables, own_vel, peer_vel, own_dif, peer_dif, step - 1, step, arch)

    sub = sublane()
    state_row = (sub & 3) == 3

    def block(j, carry):
        start = pl.multiple_of(j * WIDTH, WIDTH)
        slot = part * CHUNK + j
        for step in (1, 2):
            index = cells_of(cell_ref, step, start, sub)
            noise = stack_halves(noise_ref, (step,), start)
            moved = advance(
                tables, step - 1, tile_ref[step, 0, slot] // TILES, index, noise, sub
            )
            if step == 1:
                code = (moved * POS_SCALE).astype(jnp.int32)
                second_ref[j] = jnp.where(state_row, 0, code)
            else:
                third_ref[j] = moved
        return carry

    lax.fori_loop(0, CHUNK, block, 0, unroll=GROUP // 2)


def relay_kernel(route_ref, in_ref, add_ref, out_ref):
    def block(j, carry):
        out_ref[route_ref[1, 0, j]] = in_ref[j] + add_ref[j]
        return carry

    lax.fori_loop(0, NB, block, 0, unroll=16)


def decode(code):
    mass = ((code >> 16) + 32768).astype(jnp.float32) * (1.0 / MASS_SCALE)
    frac = (code & 65535).astype(jnp.float32) * (1.0 / FRAC_SCALE)
    return mass, frac


def histogram(tile_ref, bed_ref, dep_ref, step):
    sub = sublane()
    lanes = lax.broadcasted_iota(jnp.int32, (128, 128), 0)

    def group(i, total):
        hits = []
        weights = []
        for k in range(GROUP):
            slot = i * GROUP + k
            tile = tile_ref[step, 0, slot] // TILES
            for half in range(2):
                start = pl.multiple_of(slot * WIDTH + half * 128, 128)
                cell = bed_ref[step : step + 1, pl.ds(start, 128)]
                dep = jnp.broadcast_to(dep_ref[pl.ds(2 * slot + half, 1), :], (8, 128))
                cell = jnp.broadcast_to(cell, (8, 128))
                row = (cell >> 7) + tile * 4
                mine = jnp.where(row == sub, dep, 0.0)
                high = mine.astype(jnp.bfloat16).astype(jnp.float32)
                weights.append(jnp.concatenate([high, mine - high], axis=0).astype(jnp.bfloat16))
                column = jnp.broadcast_to((cell & 127)[0:1], (128, 128))
                hits.append(jnp.where(column == lanes, 1.0, 0.0).astype(jnp.bfloat16))
        hit = jnp.concatenate(hits, axis=1)
        weight = jnp.concatenate(weights, axis=1)
        return total + lax.dot_general(
            weight, hit, (((1,), (1,)), ((), ())), preferred_element_type=jnp.float32
        )

    total = lax.fori_loop(0, NB // GROUP, group, jnp.zeros((16, 128), jnp.float32))
    return total[0:8] + total[8:16]


def bed_first_kernel(tile_ref, bed_ref, mass_ref, settle_ref, out_ref, dep_ref):
    dep_ref[...] = mass_ref[...] * fraction(settle_ref[...])
    out_ref[...] = histogram(tile_ref, bed_ref, dep_ref, 0)


def bed_second_kernel(tile_ref, bed_ref, state_ref, before_ref, out_ref, dep_ref):
    mass, frac = decode(state_ref[pl.ds(3, 2 * NB, stride=4), :])
    dep_ref[...] = mass * (1.0 - frac) * frac
    out_ref[...] = before_ref[...] + histogram(tile_ref, bed_ref, dep_ref, 1)


def bed_third_kernel(
    tile_ref, bed_ref, state_ref, before_ref, mass_ref, own_ref, peer_ref, dep_ref
):
    mass, frac = decode(state_ref[pl.ds(3, 2 * NB, stride=4), :])
    left = mass * (1.0 - frac) * (1.0 - frac)
    dep_ref[...] = left * frac
    mass_ref[...] = left * (1.0 - frac)
    total = before_ref[...] + histogram(tile_ref, bed_ref, dep_ref, 2)
    total = total * (BEDC / PARTS)
    first = lax.axis_index("arch") == 0
    own_ref[...] = jnp.where(first, total[0:4], total[4:8])
    peer_ref[...] = jnp.where(first, total[4:8], total[0:4])


def finish_kernel(in_ref, add_ref, out_ref):
    def block(j, carry):
        start = pl.multiple_of(j * WIDTH, WIDTH)
        here = in_ref[j].astype(jnp.float32) * (1.0 / POS_SCALE) + add_ref[j]
        out_ref[:, pl.ds(start, 128)] = here[0:3]
        out_ref[:, pl.ds(start + 128, 128)] = here[4:7]
        return carry

    lax.fori_loop(0, NB, block, 0, unroll=GROUP)


def body(
    position, particle_mass, settling, walk_noise, velocity, diffusivity,
    block_tile, cell_index, bed_cell, route_code,
):
    slabs = velocity.shape[0]
    swap = [(0, 1), (1, 0)]
    vel = velocity.transpose(1, 2, 0, 3).reshape(3, slabs, CELLS)
    dif = diffusivity.transpose(1, 0, 2).reshape(slabs, CELLS)
    peer_vel = lax.ppermute(vel, "arch", swap)
    peer_dif = lax.ppermute(dif, "arch", swap)
    mass = particle_mass.reshape(2 * NB, 128)
    settle = settling.reshape(2 * NB, 128)

    state_type = jax.ShapeDtypeStruct((NB, 8, 128), jnp.int32)
    move_type = jax.ShapeDtypeStruct((NB, 8, 128), jnp.float32)
    bed_type = jax.ShapeDtypeStruct((8, 128), jnp.float32)
    steps = NB // CHUNK
    span = CHUNK * WIDTH
    dep_scratch = [pltpu.VMEM((2 * NB, 128), jnp.float32)]

    outgoing = pl.pallas_call(
        first_kernel,
        grid=(steps,),
        in_specs=[whole(SMEM), whole(SMEM), whole(), whole(), whole(), whole()]
        + [
            pl.BlockSpec((3, span), lambda i: (0, i)),
            pl.BlockSpec((2 * CHUNK, 128), lambda i: (i, 0)),
            pl.BlockSpec((2 * CHUNK, 128), lambda i: (i, 0)),
            pl.BlockSpec((1, 3, span), lambda i: (0, 0, i)),
            pl.BlockSpec((3, span), lambda i: (0, i)),
        ],
        out_specs=pl.BlockSpec((NB, 8, 128), lambda i: (0, 0, 0)),
        out_shape=state_type,
        scratch_shapes=[
            pltpu.VMEM((1, 2, ROWS, 8, 128), jnp.float32),
            pltpu.VMEM((2 * CHUNK, 128), jnp.int32),
        ],
        compiler_params=params(),
        name="first",
    )(
        block_tile, route_code, vel, peer_vel, dif, peer_dif,
        position, mass, settle, walk_noise, cell_index,
    )

    incoming = lax.all_to_all(outgoing, "dom", 0, 0, tiled=True)

    second, third = pl.pallas_call(
        later_kernel,
        grid=(steps,),
        in_specs=[whole(SMEM), whole(), whole(), whole(), whole()]
        + [
            pl.BlockSpec((3, 3, span), lambda i: (0, 0, i)),
            pl.BlockSpec((3, span), lambda i: (0, i)),
        ],
        out_specs=[pl.BlockSpec((CHUNK, 8, 128), lambda i: (i, 0, 0))] * 2,
        out_shape=[state_type, move_type],
        scratch_shapes=[pltpu.VMEM((2, 2, ROWS, 8, 128), jnp.float32)],
        compiler_params=params(),
        cost_estimate=pl.CostEstimate(flops=10**9, bytes_accessed=10**7, transcendentals=0),
        name="later",
    )(block_tile, vel, peer_vel, dif, peer_dif, walk_noise, cell_index)

    bed = pl.pallas_call(
        bed_first_kernel,
        in_specs=[whole(SMEM), whole(), whole(), whole()],
        out_specs=whole(),
        out_shape=bed_type,
        scratch_shapes=dep_scratch,
        compiler_params=params(),
        cost_estimate=pl.CostEstimate(flops=10**9, bytes_accessed=10**7, transcendentals=0),
        name="bed_first",
    )(block_tile, bed_cell, mass, settle)

    outgoing = pl.pallas_call(
        relay_kernel,
        in_specs=[whole(SMEM), whole(), whole()],
        out_specs=whole(),
        out_shape=state_type,
        compiler_params=params(),
        name="relay",
    )(route_code, incoming, second)

    bed = pl.pallas_call(
        bed_second_kernel,
        in_specs=[whole(SMEM), whole(), whole(), whole()],
        out_specs=whole(),
        out_shape=bed_type,
        scratch_shapes=dep_scratch,
        compiler_params=params(),
        cost_estimate=pl.CostEstimate(flops=10**9, bytes_accessed=10**7, transcendentals=0),
        name="bed_second",
    )(block_tile, bed_cell, incoming.reshape(8 * NB, 128), bed)

    incoming = lax.all_to_all(outgoing, "dom", 0, 0, tiled=True)

    final_mass, own, peer = pl.pallas_call(
        bed_third_kernel,
        in_specs=[whole(SMEM), whole(), whole(), whole()],
        out_specs=[whole(), whole(), whole()],
        out_shape=[
            jax.ShapeDtypeStruct((2 * NB, 128), jnp.float32),
            jax.ShapeDtypeStruct((4, 128), jnp.float32),
            jax.ShapeDtypeStruct((4, 128), jnp.float32),
        ],
        scratch_shapes=dep_scratch,
        compiler_params=params(),
        name="bed_third",
    )(block_tile, bed_cell, incoming.reshape(8 * NB, 128), bed)
    other = lax.ppermute(peer, "arch", swap)

    final_position = pl.pallas_call(
        finish_kernel,
        in_specs=[whole(), whole()],
        out_specs=whole(),
        out_shape=jax.ShapeDtypeStruct((3, PARTS), jnp.float32),
        compiler_params=params(),
        cost_estimate=pl.CostEstimate(flops=10**7, bytes_accessed=10**6, transcendentals=0),
        name="finish",
    )(incoming, third)
    return (
        final_position,
        final_mass.reshape(PARTS),
        (own + other).reshape(1, BEDC),
    )


def solution(mesh):
    one = P(("arch", "dom"))
    two = P(None, ("arch", "dom"))
    rows = P(None, ("arch", "dom"), None)
    return jax.shard_map(
        body,
        mesh=mesh,
        in_specs=(
            two, one, one, P(None, None, ("arch", "dom")),
            P(None, None, ("arch", "dom"), None), rows, rows, two, two, rows,
        ),
        out_specs=(two, one, P(("arch", "dom"), None)),
        check_vma=False,
    )
```

```python
import jax
import jax.numpy as jnp
from jax import lax
from jax.experimental import pallas as pl
from jax.experimental.pallas import tpu as pltpu
from jax.sharding import PartitionSpec as P

NB = 128
WIDTH = 256
PARTS = NB * WIDTH
CELLS = 2048
ROWS = CELLS // 128
BEDC = 512
TILES = 128
DT = 0.5
CHUNK = 64
GROUP = 32
FIRST_UNROLL = 32
LATER_UNROLL = 16

POS_SCALE = 2.0**26
MASS_SCALE = 32767.0
FRAC_SCALE = 166000.0

VMEM = pltpu.VMEM
SMEM = pltpu.SMEM


def whole(space=VMEM):
    return pl.BlockSpec(memory_space=space)


def params(mebibytes=24):
    return pltpu.CompilerParams(vmem_limit_bytes=mebibytes * 1024 * 1024)


def in_hbm(*arrays):
    return [pltpu.with_memory_space_constraint(a, pltpu.HBM) for a in arrays]


def in_vmem(kind):
    return pltpu.VMEM(kind.shape, kind.dtype)


def sublane():
    return lax.broadcasted_iota(jnp.int32, (8, 128), 0)


def fill_tables(tables, own_vel, peer_vel, own_dif, peer_dif, slot, step, arch):
    for vel, dif, tile in ((own_vel, own_dif, arch), (peer_vel, peer_dif, 1 - arch)):
        for c in range(4):
            v = (vel[c] if c < 3 else dif[...]).astype(jnp.float32)
            total = v[step : step + 1] + v[step + 1 : step + 2]
            value = 0.5 * DT * total if c < 3 else jnp.sqrt(DT * total)
            for r in range(ROWS):
                row = value[:, 128 * r : 128 * (r + 1)]
                tables[slot, tile, r, c : c + 1, :] = row
                tables[slot, tile, r, c + 4 : c + 5, :] = row


def halves(low, high, sub):
    return jnp.where(sub < 4, jnp.broadcast_to(low, (8, 128)), jnp.broadcast_to(high, (8, 128)))


def stack_halves(ref, lead, start):
    low = ref[lead + (slice(None), pl.ds(start, 128))]
    high = ref[lead + (slice(None), pl.ds(start + 128, 128))]
    gap = jnp.zeros((1, 128), jnp.float32)
    return jnp.concatenate([low, gap, high, gap], axis=0)


def advance(tables, slot, tile, index, noise, sub):
    lane = index & 127
    values = [
        jnp.take_along_axis(tables[slot, tile, r], lane, axis=1, mode="promise_in_bounds")
        for r in range(ROWS)
    ]
    bit = 128
    while len(values) > 1:
        odd = (index & bit) != 0
        values = [jnp.where(odd, b, a) for a, b in zip(values[0::2], values[1::2])]
        bit *= 2
    value = values[0]
    spread = jnp.where((sub & 3) == 3, value, 0.0)
    spread = spread + pltpu.roll(spread, 7, 0)
    spread = spread + pltpu.roll(spread, 6, 0)
    return value + spread * noise


def cells_of(cell_ref, step, start, sub):
    low = cell_ref[step : step + 1, pl.ds(start, 128)]
    high = cell_ref[step : step + 1, pl.ds(start + 128, 128)]
    return halves(low, high, sub)


def fraction(settling):
    return 1.0 - jnp.exp(-DT * settling)


def first_kernel(
    tile_ref, route_ref, own_vel, peer_vel, own_dif, peer_dif,
    pos_ref, mass_ref, settle_ref, noise_ref, cell_ref, out_ref, tables, code_ref,
):
    arch = lax.axis_index("arch")
    part = pl.program_id(0)

    @pl.when(part == 0)
    def _():
        fill_tables(tables, own_vel, peer_vel, own_dif, peer_dif, 0, 0, arch)

    mass_code = (mass_ref[...] * MASS_SCALE + 0.5).astype(jnp.int32)
    mass_code = jnp.clip(mass_code, 0, 65535) - 32768
    frac_code = (fraction(settle_ref[...]) * FRAC_SCALE + 0.5).astype(jnp.int32)
    frac_code = jnp.clip(frac_code, 0, 65535)
    code_ref[...] = mass_code * 65536 + frac_code
    sub = sublane()
    state_row = (sub & 3) == 3
    fall = jnp.where((sub & 3) == 2, -3.0 * DT, 0.0)

    def block(j, carry):
        start = pl.multiple_of(j * WIDTH, WIDTH)
        slot = part * CHUNK + j
        index = cells_of(cell_ref, 0, start, sub)
        noise = stack_halves(noise_ref, (0,), start)
        here = stack_halves(pos_ref, (), start)
        speed = halves(settle_ref[pl.ds(2 * j, 1), :], settle_ref[pl.ds(2 * j + 1, 1), :], sub)
        here = here + fall * speed
        here = here + advance(tables, 0, tile_ref[0, 0, slot] // TILES, index, noise, sub)
        state = halves(code_ref[pl.ds(2 * j, 1), :], code_ref[pl.ds(2 * j + 1, 1), :], sub)
        code = jnp.where(state_row, state, (here * POS_SCALE).astype(jnp.int32))
        out_ref[route_ref[0, 0, slot]] = code
        return carry

    lax.fori_loop(0, CHUNK, block, 0, unroll=FIRST_UNROLL)


def later_kernel(
    tile_ref, own_vel, peer_vel, own_dif, peer_dif, noise_ref, cell_ref,
    second_ref, third_ref, tables,
):
    arch = lax.axis_index("arch")
    part = pl.program_id(0)

    @pl.when(part == 0)
    def _():
        for step in (1, 2):
            fill_tables(tables, own_vel, peer_vel, own_dif, peer_dif, step - 1, step, arch)

    sub = sublane()
    state_row = (sub & 3) == 3

    def block(j, carry):
        start = pl.multiple_of(j * WIDTH, WIDTH)
        slot = part * CHUNK + j
        for step in (1, 2):
            index = cells_of(cell_ref, step, start, sub)
            noise = stack_halves(noise_ref, (step,), start)
            moved = advance(
                tables, step - 1, tile_ref[step, 0, slot] // TILES, index, noise, sub
            )
            if step == 1:
                code = (moved * POS_SCALE).astype(jnp.int32)
                second_ref[j] = jnp.where(state_row, 0, code)
            else:
                third_ref[j] = moved
        return carry

    lax.fori_loop(0, CHUNK, block, 0, unroll=LATER_UNROLL)


def relay_kernel(route_ref, in_ref, add_ref, out_ref):
    def block(j, carry):
        out_ref[route_ref[1, 0, j]] = in_ref[j] + add_ref[j]
        return carry

    lax.fori_loop(0, NB, block, 0, unroll=16)


def decode(code):
    mass = ((code >> 16) + 32768).astype(jnp.float32) * (1.0 / MASS_SCALE)
    frac = (code & 65535).astype(jnp.float32) * (1.0 / FRAC_SCALE)
    return mass, frac


def histogram(tile_ref, bed_ref, dep_ref, step):
    sub = sublane()
    lanes = lax.broadcasted_iota(jnp.int32, (128, 128), 0)

    def group(i, total):
        hits = []
        weights = []
        for k in range(GROUP):
            slot = i * GROUP + k
            tile = tile_ref[step, 0, slot] // TILES
            for half in range(2):
                start = pl.multiple_of(slot * WIDTH + half * 128, 128)
                cell = bed_ref[step : step + 1, pl.ds(start, 128)]
                dep = jnp.broadcast_to(dep_ref[pl.ds(2 * slot + half, 1), :], (8, 128))
                cell = jnp.broadcast_to(cell, (8, 128))
                row = (cell >> 7) + tile * 4
                mine = jnp.where(row == sub, dep, 0.0)
                high = mine.astype(jnp.bfloat16).astype(jnp.float32)
                weights.append(jnp.concatenate([high, mine - high], axis=0).astype(jnp.bfloat16))
                column = jnp.broadcast_to((cell & 127)[0:1], (128, 128))
                hits.append(jnp.where(column == lanes, 1.0, 0.0).astype(jnp.bfloat16))
        hit = jnp.concatenate(hits, axis=1)
        weight = jnp.concatenate(weights, axis=1)
        return total + lax.dot_general(
            weight, hit, (((1,), (1,)), ((), ())), preferred_element_type=jnp.float32
        )

    total = lax.fori_loop(0, NB // GROUP, group, jnp.zeros((16, 128), jnp.float32))
    return total[0:8] + total[8:16]


def bed_first_kernel(tile_ref, bed_ref, mass_ref, settle_ref, out_ref, dep_ref):
    dep_ref[...] = mass_ref[...] * fraction(settle_ref[...])
    out_ref[...] = histogram(tile_ref, bed_ref, dep_ref, 0)


def bed_second_kernel(tile_ref, bed_ref, state_ref, before_ref, out_ref, dep_ref):
    mass, frac = decode(state_ref[pl.ds(3, 2 * NB, stride=4), :])
    dep_ref[...] = mass * (1.0 - frac) * frac
    out_ref[...] = before_ref[...] + histogram(tile_ref, bed_ref, dep_ref, 1)


def bed_third_kernel(
    tile_ref, bed_ref, state_ref, before_ref, mass_ref, own_ref, peer_ref, dep_ref
):
    mass, frac = decode(state_ref[pl.ds(3, 2 * NB, stride=4), :])
    left = mass * (1.0 - frac) * (1.0 - frac)
    dep_ref[...] = left * frac
    mass_ref[...] = left * (1.0 - frac)
    total = before_ref[...] + histogram(tile_ref, bed_ref, dep_ref, 2)
    total = total * (BEDC / PARTS)
    first = lax.axis_index("arch") == 0
    own_ref[...] = jnp.where(first, total[0:4], total[4:8])
    peer_ref[...] = jnp.where(first, total[4:8], total[0:4])


def finish_kernel(in_ref, add_ref, out_ref):
    def block(j, carry):
        start = pl.multiple_of(j * WIDTH, WIDTH)
        here = in_ref[j].astype(jnp.float32) * (1.0 / POS_SCALE) + add_ref[j]
        out_ref[:, pl.ds(start, 128)] = here[0:3]
        out_ref[:, pl.ds(start + 128, 128)] = here[4:7]
        return carry

    lax.fori_loop(0, NB, block, 0, unroll=16)


def body(
    position, particle_mass, settling, walk_noise, velocity, diffusivity,
    block_tile, cell_index, bed_cell, route_code,
):
    slabs = velocity.shape[0]
    swap = [(0, 1), (1, 0)]
    vel = velocity.transpose(1, 2, 0, 3).reshape(3, slabs, CELLS)
    dif = diffusivity.transpose(1, 0, 2).reshape(slabs, CELLS)
    peer_vel = lax.ppermute(vel, "arch", swap)
    peer_dif = lax.ppermute(dif, "arch", swap)
    mass = particle_mass.reshape(2 * NB, 128)
    settle = settling.reshape(2 * NB, 128)

    state_type = jax.ShapeDtypeStruct((NB, 8, 128), jnp.int32)
    move_type = jax.ShapeDtypeStruct((NB, 8, 128), jnp.float32)
    bed_type = jax.ShapeDtypeStruct((8, 128), jnp.float32)
    steps = NB // CHUNK
    span = CHUNK * WIDTH
    dep_scratch = [pltpu.VMEM((2 * NB, 128), jnp.float32)]

    outgoing = pl.pallas_call(
        first_kernel,
        grid=(steps,),
        in_specs=[whole(SMEM), whole(SMEM), whole(), whole(), whole(), whole()]
        + [
            pl.BlockSpec((3, span), lambda i: (0, i)),
            pl.BlockSpec((2 * CHUNK, 128), lambda i: (i, 0)),
            pl.BlockSpec((2 * CHUNK, 128), lambda i: (i, 0)),
            pl.BlockSpec((1, 3, span), lambda i: (0, 0, i)),
            pl.BlockSpec((3, span), lambda i: (0, i)),
        ],
        out_specs=pl.BlockSpec((NB, 8, 128), lambda i: (0, 0, 0)),
        out_shape=state_type,
        scratch_shapes=[
            pltpu.VMEM((1, 2, ROWS, 8, 128), jnp.float32),
            pltpu.VMEM((2 * CHUNK, 128), jnp.int32),
        ],
        compiler_params=params(),
        name="first",
    )(
        *in_hbm(block_tile, route_code), *in_hbm(vel), peer_vel, *in_hbm(dif), peer_dif,
        *in_hbm(position, mass, settle, walk_noise, cell_index),
    )

    incoming = lax.all_to_all(outgoing, "dom", 0, 0, tiled=True)

    second, third = pl.pallas_call(
        later_kernel,
        grid=(steps,),
        in_specs=[whole(SMEM), whole(), whole(), whole(), whole()]
        + [
            pl.BlockSpec((3, 3, span), lambda i: (0, 0, i)),
            pl.BlockSpec((3, span), lambda i: (0, i)),
        ],
        out_specs=[pl.BlockSpec((CHUNK, 8, 128), lambda i: (i, 0, 0))] * 2,
        out_shape=[in_vmem(state_type), in_vmem(move_type)],
        scratch_shapes=[pltpu.VMEM((2, 2, ROWS, 8, 128), jnp.float32)],
        compiler_params=params(),
        cost_estimate=pl.CostEstimate(flops=10**9, bytes_accessed=10**7, transcendentals=0),
        name="later",
    )(*in_hbm(block_tile, vel), peer_vel, *in_hbm(dif), peer_dif, *in_hbm(walk_noise, cell_index))

    bed = pl.pallas_call(
        bed_first_kernel,
        in_specs=[whole(SMEM), whole(), whole(), whole()],
        out_specs=whole(),
        out_shape=bed_type,
        scratch_shapes=dep_scratch,
        compiler_params=params(),
        cost_estimate=pl.CostEstimate(flops=10**9, bytes_accessed=10**7, transcendentals=0),
        name="bed_first",
    )(block_tile, bed_cell, mass, settle)

    outgoing = pl.pallas_call(
        relay_kernel,
        in_specs=[whole(SMEM), whole(), whole()],
        out_specs=whole(),
        out_shape=state_type,
        compiler_params=params(),
        name="relay",
    )(route_code, incoming, second)

    bed = pl.pallas_call(
        bed_second_kernel,
        in_specs=[whole(SMEM), whole(), whole(), whole()],
        out_specs=whole(),
        out_shape=bed_type,
        scratch_shapes=dep_scratch,
        compiler_params=params(),
        cost_estimate=pl.CostEstimate(flops=10**9, bytes_accessed=10**7, transcendentals=0),
        name="bed_second",
    )(block_tile, bed_cell, incoming.reshape(8 * NB, 128), bed)

    incoming = lax.all_to_all(outgoing, "dom", 0, 0, tiled=True)

    final_mass, own, peer = pl.pallas_call(
        bed_third_kernel,
        in_specs=[whole(SMEM), whole(), whole(), whole()],
        out_specs=[whole(), whole(), whole()],
        out_shape=[
            jax.ShapeDtypeStruct((2 * NB, 128), jnp.float32),
            jax.ShapeDtypeStruct((4, 128), jnp.float32),
            jax.ShapeDtypeStruct((4, 128), jnp.float32),
        ],
        scratch_shapes=dep_scratch,
        compiler_params=params(),
        name="bed_third",
    )(block_tile, bed_cell, incoming.reshape(8 * NB, 128), bed)
    other = lax.ppermute(peer, "arch", swap)

    final_position = pl.pallas_call(
        finish_kernel,
        in_specs=[whole(), whole()],
        out_specs=whole(),
        out_shape=jax.ShapeDtypeStruct((3, PARTS), jnp.float32),
        compiler_params=params(),
        cost_estimate=pl.CostEstimate(flops=10**7, bytes_accessed=10**6, transcendentals=0),
        name="finish",
    )(incoming, third)
    return (
        final_position,
        final_mass.reshape(PARTS),
        (own + other).reshape(1, BEDC),
    )


def solution(mesh):
    one = P(("arch", "dom"))
    two = P(None, ("arch", "dom"))
    rows = P(None, ("arch", "dom"), None)
    return jax.shard_map(
        body,
        mesh=mesh,
        in_specs=(
            two, one, one, P(None, None, ("arch", "dom")),
            P(None, None, ("arch", "dom"), None), rows, rows, two, two, rows,
        ),
        out_specs=(two, one, P(("arch", "dom"), None)),
        check_vma=False,
    )
```

```python
import jax
import jax.numpy as jnp
from jax import lax
from jax.experimental import pallas as pl
from jax.experimental.pallas import tpu as pltpu
from jax.sharding import PartitionSpec as P

NB = 128
WIDTH = 256
PARTS = NB * WIDTH
CELLS = 2048
ROWS = CELLS // 128
BEDC = 512
TILES = 128
DT = 0.5
CHUNK = 64
GROUP = 32
FIRST_UNROLL = 32
LATER_UNROLL = 16

POS_SCALE = 2.0**26
MASS_SCALE = 32767.0
FRAC_SCALE = 166000.0

VMEM = pltpu.VMEM
SMEM = pltpu.SMEM


def whole(space=VMEM):
    return pl.BlockSpec(memory_space=space)


def params(mebibytes=24):
    return pltpu.CompilerParams(vmem_limit_bytes=mebibytes * 1024 * 1024)


def in_hbm(*arrays):
    return [pltpu.with_memory_space_constraint(a, pltpu.HBM) for a in arrays]


def in_vmem(kind):
    return pltpu.VMEM(kind.shape, kind.dtype)


def sublane():
    return lax.broadcasted_iota(jnp.int32, (8, 128), 0)


def fill_tables(tables, own_vel, peer_vel, own_dif, peer_dif, slot, step, arch):
    for vel, dif, tile in ((own_vel, own_dif, arch), (peer_vel, peer_dif, 1 - arch)):
        for c in range(4):
            v = (vel[c] if c < 3 else dif[...]).astype(jnp.float32)
            total = v[step : step + 1] + v[step + 1 : step + 2]
            value = 0.5 * DT * total if c < 3 else jnp.sqrt(DT * total)
            for r in range(ROWS):
                row = value[:, 128 * r : 128 * (r + 1)]
                tables[slot, tile, r, c : c + 1, :] = row
                tables[slot, tile, r, c + 4 : c + 5, :] = row


def halves(low, high, sub):
    return jnp.where(sub < 4, jnp.broadcast_to(low, (8, 128)), jnp.broadcast_to(high, (8, 128)))


def stack_halves(ref, lead, start):
    low = ref[lead + (slice(None), pl.ds(start, 128))]
    high = ref[lead + (slice(None), pl.ds(start + 128, 128))]
    gap = jnp.zeros((1, 128), jnp.float32)
    return jnp.concatenate([low, gap, high, gap], axis=0)


def advance(tables, slot, tile, index, noise, sub):
    lane = index & 127
    values = [
        jnp.take_along_axis(tables[slot, tile, r], lane, axis=1, mode="promise_in_bounds")
        for r in range(ROWS)
    ]
    bit = 128
    while len(values) > 1:
        odd = (index & bit) != 0
        values = [jnp.where(odd, b, a) for a, b in zip(values[0::2], values[1::2])]
        bit *= 2
    value = values[0]
    spread = jnp.where((sub & 3) == 3, value, 0.0)
    spread = spread + pltpu.roll(spread, 7, 0)
    spread = spread + pltpu.roll(spread, 6, 0)
    return value + spread * noise


def cells_of(cell_ref, step, start, sub):
    low = cell_ref[step : step + 1, pl.ds(start, 128)]
    high = cell_ref[step : step + 1, pl.ds(start + 128, 128)]
    return halves(low, high, sub)


def fraction(settling):
    return 1.0 - jnp.exp(-DT * settling)


def first_kernel(
    tile_ref, route_ref, own_vel, peer_vel, own_dif, peer_dif,
    pos_ref, mass_ref, settle_ref, noise_ref, cell_ref, out_ref, tables, code_ref,
):
    arch = lax.axis_index("arch")
    part = pl.program_id(0)

    @pl.when(part == 0)
    def _():
        fill_tables(tables, own_vel, peer_vel, own_dif, peer_dif, 0, 0, arch)

    mass_code = (mass_ref[...] * MASS_SCALE + 0.5).astype(jnp.int32)
    mass_code = jnp.clip(mass_code, 0, 65535) - 32768
    frac_code = (fraction(settle_ref[...]) * FRAC_SCALE + 0.5).astype(jnp.int32)
    frac_code = jnp.clip(frac_code, 0, 65535)
    code_ref[...] = mass_code * 65536 + frac_code
    sub = sublane()
    state_row = (sub & 3) == 3
    fall = jnp.where((sub & 3) == 2, -3.0 * DT, 0.0)

    def block(j, carry):
        start = pl.multiple_of(j * WIDTH, WIDTH)
        slot = part * CHUNK + j
        index = cells_of(cell_ref, 0, start, sub)
        noise = stack_halves(noise_ref, (0,), start)
        here = stack_halves(pos_ref, (), start)
        speed = halves(settle_ref[pl.ds(2 * j, 1), :], settle_ref[pl.ds(2 * j + 1, 1), :], sub)
        here = here + fall * speed
        here = here + advance(tables, 0, tile_ref[0, 0, slot] // TILES, index, noise, sub)
        state = halves(code_ref[pl.ds(2 * j, 1), :], code_ref[pl.ds(2 * j + 1, 1), :], sub)
        code = jnp.where(state_row, state, (here * POS_SCALE).astype(jnp.int32))
        out_ref[route_ref[0, 0, slot]] = code
        return carry

    lax.fori_loop(0, CHUNK, block, 0, unroll=FIRST_UNROLL)


def later_kernel(
    tile_ref, own_vel, peer_vel, own_dif, peer_dif, noise_ref, cell_ref,
    second_ref, third_ref, tables,
):
    arch = lax.axis_index("arch")
    part = pl.program_id(0)

    @pl.when(part == 0)
    def _():
        for step in (1, 2):
            fill_tables(tables, own_vel, peer_vel, own_dif, peer_dif, step - 1, step, arch)

    sub = sublane()
    state_row = (sub & 3) == 3

    def block(j, carry):
        start = pl.multiple_of(j * WIDTH, WIDTH)
        slot = part * CHUNK + j
        for step in (1, 2):
            index = cells_of(cell_ref, step, start, sub)
            noise = stack_halves(noise_ref, (step,), start)
            moved = advance(
                tables, step - 1, tile_ref[step, 0, slot] // TILES, index, noise, sub
            )
            if step == 1:
                code = (moved * POS_SCALE).astype(jnp.int32)
                second_ref[j] = jnp.where(state_row, 0, code)
            else:
                third_ref[j] = moved
        return carry

    lax.fori_loop(0, CHUNK, block, 0, unroll=LATER_UNROLL)


def relay_kernel(route_ref, in_ref, add_ref, out_ref):
    def block(j, carry):
        out_ref[route_ref[1, 0, j]] = in_ref[j] + add_ref[j]
        return carry

    lax.fori_loop(0, NB, block, 0, unroll=16)


def decode(code):
    mass = ((code >> 16) + 32768).astype(jnp.float32) * (1.0 / MASS_SCALE)
    frac = (code & 65535).astype(jnp.float32) * (1.0 / FRAC_SCALE)
    return mass, frac


def split_cells(tile_ref, bed_ref, step, row_ref, column_ref):
    def block(slot, carry):
        tile = tile_ref[step, 0, slot] // TILES
        for half in range(2):
            start = pl.multiple_of(slot * WIDTH + half * 128, 128)
            cell = bed_ref[step : step + 1, pl.ds(start, 128)]
            run = pl.ds(2 * slot + half, 1)
            row_ref[run, :] = ((cell >> 6) + tile * 8).astype(jnp.float32)
            column_ref[run, :] = (cell & 63).astype(jnp.float32)
        return carry

    lax.fori_loop(0, NB, block, 0, unroll=16)


def spread_run(ref, run):
    row = jnp.broadcast_to(ref[pl.ds(run, 1), :], (8, 128))
    return jnp.concatenate([row, row], axis=0).astype(jnp.bfloat16)


def histogram(row_ref, column_ref, dep, high_ref, rest_ref, lay_ref):
    high = dep.astype(jnp.bfloat16).astype(jnp.float32)
    high_ref[...] = high
    rest_ref[...] = dep - high
    places = lax.broadcasted_iota(jnp.int32, (64, 128), 0).astype(jnp.float32).astype(jnp.bfloat16)
    one, zero = jnp.bfloat16(1), jnp.bfloat16(0)

    def group(i, total):
        hits = []
        weights = []
        for k in range(2 * GROUP):
            run = 2 * GROUP * i + k
            mine = spread_run(row_ref, run) == places[0:16]
            parts = [jnp.where(mine, spread_run(ref, run), zero) for ref in (high_ref, rest_ref)]
            weights.append(jnp.concatenate(parts, axis=0))
            column = jnp.concatenate([spread_run(column_ref, run)] * 4, axis=0)
            hits.append(jnp.where(column == places, one, zero))
        weight = jnp.concatenate(weights, axis=1)
        hit = jnp.concatenate(hits, axis=1)
        return total + lax.dot_general(
            weight, hit, (((1,), (1,)), ((), ())), preferred_element_type=jnp.float32
        )

    total = lax.fori_loop(0, NB // GROUP, group, jnp.zeros((32, 64), jnp.float32), unroll=4)
    lay_ref[:, 0:64] = total[0:16] + total[16:32]
    return jnp.concatenate([lay_ref[pl.ds(i, 8, stride=2), 0:64] for i in range(2)], axis=1)


def bed_first_kernel(
    tile_ref, bed_ref, mass_ref, settle_ref, out_ref, row_ref, column_ref, *scratch
):
    split_cells(tile_ref, bed_ref, 0, row_ref, column_ref)
    dep = mass_ref[...] * fraction(settle_ref[...])
    out_ref[...] = histogram(row_ref, column_ref, dep, *scratch)


def bed_second_kernel(
    tile_ref, bed_ref, state_ref, before_ref, out_ref, next_row_ref, next_column_ref,
    row_ref, column_ref, *scratch,
):
    split_cells(tile_ref, bed_ref, 1, row_ref, column_ref)
    split_cells(tile_ref, bed_ref, 2, next_row_ref, next_column_ref)
    mass, frac = decode(state_ref[pl.ds(3, 2 * NB, stride=4), :])
    dep = mass * (1.0 - frac) * frac
    out_ref[...] = before_ref[...] + histogram(row_ref, column_ref, dep, *scratch)


def bed_third_kernel(
    row_ref, column_ref, state_ref, before_ref, mass_ref, own_ref, peer_ref, *scratch
):
    mass, frac = decode(state_ref[pl.ds(3, 2 * NB, stride=4), :])
    left = mass * (1.0 - frac) * (1.0 - frac)
    mass_ref[...] = left * (1.0 - frac)
    total = before_ref[...] + histogram(row_ref, column_ref, left * frac, *scratch)
    total = total * (BEDC / PARTS)
    first = lax.axis_index("arch") == 0
    own_ref[...] = jnp.where(first, total[0:4], total[4:8])
    peer_ref[...] = jnp.where(first, total[4:8], total[0:4])


def finish_kernel(in_ref, add_ref, out_ref):
    def block(j, carry):
        start = pl.multiple_of(j * WIDTH, WIDTH)
        here = in_ref[j].astype(jnp.float32) * (1.0 / POS_SCALE) + add_ref[j]
        out_ref[:, pl.ds(start, 128)] = here[0:3]
        out_ref[:, pl.ds(start + 128, 128)] = here[4:7]
        return carry

    lax.fori_loop(0, NB, block, 0, unroll=16)


def body(
    position, particle_mass, settling, walk_noise, velocity, diffusivity,
    block_tile, cell_index, bed_cell, route_code,
):
    slabs = velocity.shape[0]
    swap = [(0, 1), (1, 0)]
    vel = velocity.transpose(1, 2, 0, 3).reshape(3, slabs, CELLS)
    dif = diffusivity.transpose(1, 0, 2).reshape(slabs, CELLS)
    peer_vel = lax.ppermute(vel, "arch", swap)
    peer_dif = lax.ppermute(dif, "arch", swap)
    mass = particle_mass.reshape(2 * NB, 128)
    settle = settling.reshape(2 * NB, 128)

    state_type = jax.ShapeDtypeStruct((NB, 8, 128), jnp.int32)
    move_type = jax.ShapeDtypeStruct((NB, 8, 128), jnp.float32)
    bed_type = jax.ShapeDtypeStruct((8, 128), jnp.float32)
    steps = NB // CHUNK
    span = CHUNK * WIDTH
    runs = jax.ShapeDtypeStruct((2 * NB, 128), jnp.float32)
    bed_scratch = [in_vmem(runs), in_vmem(runs), pltpu.VMEM((16, 128), jnp.float32)]

    outgoing = pl.pallas_call(
        first_kernel,
        grid=(steps,),
        in_specs=[whole(SMEM), whole(SMEM), whole(), whole(), whole(), whole()]
        + [
            pl.BlockSpec((3, span), lambda i: (0, i)),
            pl.BlockSpec((2 * CHUNK, 128), lambda i: (i, 0)),
            pl.BlockSpec((2 * CHUNK, 128), lambda i: (i, 0)),
            pl.BlockSpec((1, 3, span), lambda i: (0, 0, i)),
            pl.BlockSpec((3, span), lambda i: (0, i)),
        ],
        out_specs=pl.BlockSpec((NB, 8, 128), lambda i: (0, 0, 0)),
        out_shape=state_type,
        scratch_shapes=[
            pltpu.VMEM((1, 2, ROWS, 8, 128), jnp.float32),
            pltpu.VMEM((2 * CHUNK, 128), jnp.int32),
        ],
        compiler_params=params(),
        name="first",
    )(
        *in_hbm(block_tile, route_code), *in_hbm(vel), peer_vel, *in_hbm(dif), peer_dif,
        *in_hbm(position, mass, settle, walk_noise, cell_index),
    )

    incoming = lax.all_to_all(outgoing, "dom", 0, 0, tiled=True)

    second, third = pl.pallas_call(
        later_kernel,
        grid=(steps,),
        in_specs=[whole(SMEM), whole(), whole(), whole(), whole()]
        + [
            pl.BlockSpec((3, 3, span), lambda i: (0, 0, i)),
            pl.BlockSpec((3, span), lambda i: (0, i)),
        ],
        out_specs=[pl.BlockSpec((CHUNK, 8, 128), lambda i: (i, 0, 0))] * 2,
        out_shape=[in_vmem(state_type), in_vmem(move_type)],
        scratch_shapes=[pltpu.VMEM((2, 2, ROWS, 8, 128), jnp.float32)],
        compiler_params=params(),
        cost_estimate=pl.CostEstimate(flops=10**9, bytes_accessed=10**7, transcendentals=0),
        name="later",
    )(*in_hbm(block_tile, vel), peer_vel, *in_hbm(dif), peer_dif, *in_hbm(walk_noise, cell_index))

    bed = pl.pallas_call(
        bed_first_kernel,
        in_specs=[whole(SMEM), whole(), whole(), whole()],
        out_specs=whole(),
        out_shape=bed_type,
        scratch_shapes=[in_vmem(runs), in_vmem(runs)] + bed_scratch,
        compiler_params=params(),
        cost_estimate=pl.CostEstimate(flops=10**9, bytes_accessed=10**7, transcendentals=0),
        name="bed_first",
    )(block_tile, bed_cell, mass, settle)

    outgoing = pl.pallas_call(
        relay_kernel,
        in_specs=[whole(SMEM), whole(), whole()],
        out_specs=whole(),
        out_shape=state_type,
        compiler_params=params(),
        name="relay",
    )(route_code, incoming, second)

    bed, row, column = pl.pallas_call(
        bed_second_kernel,
        in_specs=[whole(SMEM), whole(), whole(), whole()],
        out_specs=[whole(), whole(), whole()],
        out_shape=[bed_type, in_vmem(runs), in_vmem(runs)],
        scratch_shapes=[in_vmem(runs), in_vmem(runs)] + bed_scratch,
        compiler_params=params(),
        cost_estimate=pl.CostEstimate(flops=10**9, bytes_accessed=10**7, transcendentals=0),
        name="bed_second",
    )(block_tile, bed_cell, incoming.reshape(8 * NB, 128), bed)

    incoming = lax.all_to_all(outgoing, "dom", 0, 0, tiled=True)

    final_mass, own, peer = pl.pallas_call(
        bed_third_kernel,
        in_specs=[whole()] * 4,
        out_specs=[whole(), whole(), whole()],
        out_shape=[
            jax.ShapeDtypeStruct((2 * NB, 128), jnp.float32),
            jax.ShapeDtypeStruct((4, 128), jnp.float32),
            jax.ShapeDtypeStruct((4, 128), jnp.float32),
        ],
        scratch_shapes=bed_scratch,
        compiler_params=params(),
        name="bed_third",
    )(row, column, incoming.reshape(8 * NB, 128), bed)
    other = lax.ppermute(peer, "arch", swap)

    final_position = pl.pallas_call(
        finish_kernel,
        in_specs=[whole(), whole()],
        out_specs=whole(),
        out_shape=jax.ShapeDtypeStruct((3, PARTS), jnp.float32),
        compiler_params=params(),
        cost_estimate=pl.CostEstimate(flops=10**7, bytes_accessed=10**6, transcendentals=0),
        name="finish",
    )(incoming, third)
    return (
        final_position,
        final_mass.reshape(PARTS),
        (own + other).reshape(1, BEDC),
    )


def solution(mesh):
    one = P(("arch", "dom"))
    two = P(None, ("arch", "dom"))
    rows = P(None, ("arch", "dom"), None)
    return jax.shard_map(
        body,
        mesh=mesh,
        in_specs=(
            two, one, one, P(None, None, ("arch", "dom")),
            P(None, None, ("arch", "dom"), None), rows, rows, two, two, rows,
        ),
        out_specs=(two, one, P(("arch", "dom"), None)),
        check_vma=False,
    )
```

```python
import jax
import jax.numpy as jnp
from jax import lax
from jax.experimental import pallas as pl
from jax.experimental.pallas import tpu as pltpu
from jax.sharding import PartitionSpec as P

NB = 128
WIDTH = 256
PARTS = NB * WIDTH
CELLS = 2048
ROWS = CELLS // 128
BEDC = 512
TILES = 128
DT = 0.5
CHUNK = 64
GROUP = 32
FIRST_UNROLL = 32
LATER_UNROLL = 16

LINES = 6
FIRST_CODE = (16.0, 2.0**16)
SECOND_CODE = (24.0, 43690.0)
MASS_SCALE = 32767.0
FRAC_SCALE = 166000.0

VMEM = pltpu.VMEM
SMEM = pltpu.SMEM


def whole(space=VMEM):
    return pl.BlockSpec(memory_space=space)


def params(mebibytes=24):
    return pltpu.CompilerParams(vmem_limit_bytes=mebibytes * 1024 * 1024)


def in_hbm(*arrays):
    return [pltpu.with_memory_space_constraint(a, pltpu.HBM) for a in arrays]


def in_vmem(kind):
    return pltpu.VMEM(kind.shape, kind.dtype)


def sublane():
    return lax.broadcasted_iota(jnp.int32, (8, 128), 0)


def fill_tables(tables, own_vel, peer_vel, own_dif, peer_dif, slot, step, arch):
    for vel, dif, tile in ((own_vel, own_dif, arch), (peer_vel, peer_dif, 1 - arch)):
        for c in range(4):
            v = (vel[c] if c < 3 else dif[...]).astype(jnp.float32)
            total = v[step : step + 1] + v[step + 1 : step + 2]
            value = 0.5 * DT * total if c < 3 else jnp.sqrt(DT * total)
            for r in range(ROWS):
                row = value[:, 128 * r : 128 * (r + 1)]
                for at in (c, c + 3) if c < 3 else (6, 7):
                    tables[slot, tile, r, at : at + 1, :] = row


def halves(low, high, sub):
    of_low = (sub < 3) | (sub == 6)
    return jnp.where(of_low, jnp.broadcast_to(low, (8, 128)), jnp.broadcast_to(high, (8, 128)))


def stack_halves(ref, lead, start):
    low = ref[lead + (slice(None), pl.ds(start, 128))]
    high = ref[lead + (slice(None), pl.ds(start + 128, 128))]
    return jnp.concatenate([low, high, jnp.zeros((2, 128), jnp.float32)], axis=0)


def is_z(sub):
    return (sub == 2) | (sub == 5)


def encode(here, state, code, sub):
    offset, scale = code
    scales = jnp.where(is_z(sub), 2.0 * scale, scale)
    number = (here * scales + (offset * scales + 0.5)).astype(jnp.int32)
    upper = pltpu.roll(number, 6, 0) >> 11
    lower = pltpu.roll(number, 7, 0) & 2047
    word = (number << 11) | jnp.where((sub == 0) | (sub == 3), upper, lower)
    return jnp.where(is_z(sub), state, word)


def load_block(ref, j):
    rows = ref[pl.ds(LINES * j, LINES), :]
    return jnp.concatenate([rows, jnp.zeros((2, 128), jnp.int32)], axis=0)


def decode_position(word, code, sub):
    offset, scale = code
    shares = word & 2047
    z = (pltpu.roll(shares, 2, 0) << 11) | pltpu.roll(shares, 1, 0)
    number = jnp.where(is_z(sub), z, (word >> 11) & (2**21 - 1))
    return number.astype(jnp.float32) * jnp.where(is_z(sub), 0.5 / scale, 1.0 / scale) - offset


def advance(tables, slot, tile, index, noise, sub):
    lane = index & 127
    values = [
        jnp.take_along_axis(tables[slot, tile, r], lane, axis=1, mode="promise_in_bounds")
        for r in range(ROWS)
    ]
    bit = 128
    while len(values) > 1:
        odd = (index & bit) != 0
        values = [jnp.where(odd, b, a) for a, b in zip(values[0::2], values[1::2])]
        bit *= 2
    value = values[0]
    spread = jnp.take_along_axis(
        value, jnp.where(sub < 3, 6, 7), axis=0, mode="promise_in_bounds"
    )
    return value + spread * noise


def cells_of(cell_ref, step, start, sub):
    low = cell_ref[step : step + 1, pl.ds(start, 128)]
    high = cell_ref[step : step + 1, pl.ds(start + 128, 128)]
    return halves(low, high, sub)


def fraction(settling):
    return 1.0 - jnp.exp(-DT * settling)


def first_kernel(
    tile_ref, route_ref, own_vel, peer_vel, own_dif, peer_dif,
    pos_ref, mass_ref, settle_ref, noise_ref, cell_ref, out_ref, tables, code_ref,
):
    arch = lax.axis_index("arch")
    part = pl.program_id(0)

    @pl.when(part == 0)
    def _():
        fill_tables(tables, own_vel, peer_vel, own_dif, peer_dif, 0, 0, arch)

    mass_code = (mass_ref[...] * MASS_SCALE + 0.5).astype(jnp.int32)
    mass_code = jnp.clip(mass_code, 0, 65535) - 32768
    frac_code = (fraction(settle_ref[...]) * FRAC_SCALE + 0.5).astype(jnp.int32)
    frac_code = jnp.clip(frac_code, 0, 65535)
    code_ref[...] = mass_code * 65536 + frac_code
    sub = sublane()
    fall = jnp.where(is_z(sub), -3.0 * DT, 0.0)

    def block(j, carry):
        start = pl.multiple_of(j * WIDTH, WIDTH)
        slot = part * CHUNK + j
        index = cells_of(cell_ref, 0, start, sub)
        noise = stack_halves(noise_ref, (0,), start)
        here = stack_halves(pos_ref, (), start)
        speed = halves(settle_ref[pl.ds(2 * j, 1), :], settle_ref[pl.ds(2 * j + 1, 1), :], sub)
        here = here + fall * speed
        here = here + advance(tables, 0, tile_ref[0, 0, slot] // TILES, index, noise, sub)
        state = halves(code_ref[pl.ds(2 * j, 1), :], code_ref[pl.ds(2 * j + 1, 1), :], sub)
        word = encode(here, state, FIRST_CODE, sub)
        out_ref[pl.ds(LINES * route_ref[0, 0, slot], LINES), :] = word[0:LINES]
        return carry

    lax.fori_loop(0, CHUNK, block, 0, unroll=FIRST_UNROLL)


def later_kernel(
    tile_ref, own_vel, peer_vel, own_dif, peer_dif, noise_ref, cell_ref,
    second_ref, third_ref, tables,
):
    arch = lax.axis_index("arch")
    part = pl.program_id(0)

    @pl.when(part == 0)
    def _():
        for step in (1, 2):
            fill_tables(tables, own_vel, peer_vel, own_dif, peer_dif, step - 1, step, arch)

    sub = sublane()

    def block(j, carry):
        start = pl.multiple_of(j * WIDTH, WIDTH)
        slot = part * CHUNK + j
        for step in (1, 2):
            index = cells_of(cell_ref, step, start, sub)
            noise = stack_halves(noise_ref, (step,), start)
            out_ref = second_ref if step == 1 else third_ref
            out_ref[j] = advance(
                tables, step - 1, tile_ref[step, 0, slot] // TILES, index, noise, sub
            )
        return carry

    lax.fori_loop(0, CHUNK, block, 0, unroll=LATER_UNROLL)


def relay_kernel(route_ref, in_ref, add_ref, out_ref):
    sub = sublane()

    def block(j, carry):
        word = load_block(in_ref, j)
        here = decode_position(word, FIRST_CODE, sub) + add_ref[j]
        word = encode(here, word, SECOND_CODE, sub)
        out_ref[pl.ds(LINES * route_ref[1, 0, j], LINES), :] = word[0:LINES]
        return carry

    lax.fori_loop(0, NB, block, 0, unroll=16)


def decode(code):
    mass = ((code >> 16) + 32768).astype(jnp.float32) * (1.0 / MASS_SCALE)
    frac = (code & 65535).astype(jnp.float32) * (1.0 / FRAC_SCALE)
    return mass, frac


def split_cells(tile_ref, bed_ref, step, row_ref, column_ref):
    def block(slot, carry):
        tile = tile_ref[step, 0, slot] // TILES
        for half in range(2):
            start = pl.multiple_of(slot * WIDTH + half * 128, 128)
            cell = bed_ref[step : step + 1, pl.ds(start, 128)]
            run = pl.ds(2 * slot + half, 1)
            row_ref[run, :] = ((cell >> 6) + tile * 8).astype(jnp.float32)
            column_ref[run, :] = (cell & 63).astype(jnp.float32)
        return carry

    lax.fori_loop(0, NB, block, 0, unroll=16)


def spread_run(ref, run):
    row = jnp.broadcast_to(ref[pl.ds(run, 1), :], (8, 128))
    return jnp.concatenate([row, row], axis=0).astype(jnp.bfloat16)


def histogram(row_ref, column_ref, dep, high_ref, rest_ref, lay_ref):
    high = dep.astype(jnp.bfloat16).astype(jnp.float32)
    high_ref[...] = high
    rest_ref[...] = dep - high
    places = lax.broadcasted_iota(jnp.int32, (64, 128), 0).astype(jnp.float32).astype(jnp.bfloat16)
    one, zero = jnp.bfloat16(1), jnp.bfloat16(0)

    def group(i, total):
        hits = []
        weights = []
        for k in range(2 * GROUP):
            run = 2 * GROUP * i + k
            mine = spread_run(row_ref, run) == places[0:16]
            parts = [jnp.where(mine, spread_run(ref, run), zero) for ref in (high_ref, rest_ref)]
            weights.append(jnp.concatenate(parts, axis=0))
            column = jnp.concatenate([spread_run(column_ref, run)] * 4, axis=0)
            hits.append(jnp.where(column == places, one, zero))
        weight = jnp.concatenate(weights, axis=1)
        hit = jnp.concatenate(hits, axis=1)
        return total + lax.dot_general(
            weight, hit, (((1,), (1,)), ((), ())), preferred_element_type=jnp.float32
        )

    total = lax.fori_loop(0, NB // GROUP, group, jnp.zeros((32, 64), jnp.float32), unroll=4)
    lay_ref[:, 0:64] = total[0:16] + total[16:32]
    return jnp.concatenate([lay_ref[pl.ds(i, 8, stride=2), 0:64] for i in range(2)], axis=1)


def bed_first_kernel(
    tile_ref, bed_ref, mass_ref, settle_ref, out_ref, row_ref, column_ref, *scratch
):
    split_cells(tile_ref, bed_ref, 0, row_ref, column_ref)
    dep = mass_ref[...] * fraction(settle_ref[...])
    out_ref[...] = histogram(row_ref, column_ref, dep, *scratch)


def bed_second_kernel(
    tile_ref, bed_ref, state_ref, before_ref, out_ref, next_row_ref, next_column_ref,
    row_ref, column_ref, *scratch,
):
    split_cells(tile_ref, bed_ref, 1, row_ref, column_ref)
    split_cells(tile_ref, bed_ref, 2, next_row_ref, next_column_ref)
    mass, frac = decode(state_ref[pl.ds(2, 2 * NB, stride=3), :])
    dep = mass * (1.0 - frac) * frac
    out_ref[...] = before_ref[...] + histogram(row_ref, column_ref, dep, *scratch)


def bed_third_kernel(
    row_ref, column_ref, state_ref, before_ref, mass_ref, own_ref, peer_ref, *scratch
):
    mass, frac = decode(state_ref[pl.ds(2, 2 * NB, stride=3), :])
    left = mass * (1.0 - frac) * (1.0 - frac)
    mass_ref[...] = left * (1.0 - frac)
    total = before_ref[...] + histogram(row_ref, column_ref, left * frac, *scratch)
    total = total * (BEDC / PARTS)
    first = lax.axis_index("arch") == 0
    own_ref[...] = jnp.where(first, total[0:4], total[4:8])
    peer_ref[...] = jnp.where(first, total[4:8], total[0:4])


def finish_kernel(in_ref, add_ref, out_ref):
    sub = sublane()

    def block(j, carry):
        start = pl.multiple_of(j * WIDTH, WIDTH)
        here = decode_position(load_block(in_ref, j), SECOND_CODE, sub) + add_ref[j]
        out_ref[:, pl.ds(start, 128)] = here[0:3]
        out_ref[:, pl.ds(start + 128, 128)] = here[3:6]
        return carry

    lax.fori_loop(0, NB, block, 0, unroll=16)


def exchange(outgoing):
    blocks = outgoing.reshape(NB, 1, LINES * 128)
    return lax.all_to_all(blocks, "dom", 0, 0, tiled=True).reshape(LINES * NB, 128)


def body(
    position, particle_mass, settling, walk_noise, velocity, diffusivity,
    block_tile, cell_index, bed_cell, route_code,
):
    slabs = velocity.shape[0]
    swap = [(0, 1), (1, 0)]
    vel = velocity.transpose(1, 2, 0, 3).reshape(3, slabs, CELLS)
    dif = diffusivity.transpose(1, 0, 2).reshape(slabs, CELLS)
    peer_vel = lax.ppermute(vel, "arch", swap)
    peer_dif = lax.ppermute(dif, "arch", swap)
    mass = particle_mass.reshape(2 * NB, 128)
    settle = settling.reshape(2 * NB, 128)

    state_type = jax.ShapeDtypeStruct((LINES * NB, 128), jnp.int32)
    move_type = jax.ShapeDtypeStruct((NB, 8, 128), jnp.float32)
    bed_type = jax.ShapeDtypeStruct((8, 128), jnp.float32)
    steps = NB // CHUNK
    span = CHUNK * WIDTH
    runs = jax.ShapeDtypeStruct((2 * NB, 128), jnp.float32)
    bed_scratch = [in_vmem(runs), in_vmem(runs), pltpu.VMEM((16, 128), jnp.float32)]

    outgoing = pl.pallas_call(
        first_kernel,
        grid=(steps,),
        in_specs=[whole(SMEM), whole(SMEM), whole(), whole(), whole(), whole()]
        + [
            pl.BlockSpec((3, span), lambda i: (0, i)),
            pl.BlockSpec((2 * CHUNK, 128), lambda i: (i, 0)),
            pl.BlockSpec((2 * CHUNK, 128), lambda i: (i, 0)),
            pl.BlockSpec((1, 3, span), lambda i: (0, 0, i)),
            pl.BlockSpec((3, span), lambda i: (0, i)),
        ],
        out_specs=pl.BlockSpec((LINES * NB, 128), lambda i: (0, 0)),
        out_shape=state_type,
        scratch_shapes=[
            pltpu.VMEM((1, 2, ROWS, 8, 128), jnp.float32),
            pltpu.VMEM((2 * CHUNK, 128), jnp.int32),
        ],
        compiler_params=params(),
        name="first",
    )(
        *in_hbm(block_tile, route_code), *in_hbm(vel), peer_vel, *in_hbm(dif), peer_dif,
        *in_hbm(position, mass, settle, walk_noise, cell_index),
    )

    incoming = exchange(outgoing)

    second, third = pl.pallas_call(
        later_kernel,
        grid=(steps,),
        in_specs=[whole(SMEM), whole(), whole(), whole(), whole()]
        + [
            pl.BlockSpec((3, 3, span), lambda i: (0, 0, i)),
            pl.BlockSpec((3, span), lambda i: (0, i)),
        ],
        out_specs=[pl.BlockSpec((CHUNK, 8, 128), lambda i: (i, 0, 0))] * 2,
        out_shape=[in_vmem(move_type), in_vmem(move_type)],
        scratch_shapes=[pltpu.VMEM((2, 2, ROWS, 8, 128), jnp.float32)],
        compiler_params=params(),
        cost_estimate=pl.CostEstimate(flops=10**9, bytes_accessed=10**7, transcendentals=0),
        name="later",
    )(*in_hbm(block_tile, vel), peer_vel, *in_hbm(dif), peer_dif, *in_hbm(walk_noise, cell_index))

    bed = pl.pallas_call(
        bed_first_kernel,
        in_specs=[whole(SMEM), whole(), whole(), whole()],
        out_specs=whole(),
        out_shape=bed_type,
        scratch_shapes=[in_vmem(runs), in_vmem(runs)] + bed_scratch,
        compiler_params=params(),
        cost_estimate=pl.CostEstimate(flops=10**9, bytes_accessed=10**7, transcendentals=0),
        name="bed_first",
    )(block_tile, bed_cell, mass, settle)

    outgoing = pl.pallas_call(
        relay_kernel,
        in_specs=[whole(SMEM), whole(), whole()],
        out_specs=whole(),
        out_shape=state_type,
        compiler_params=params(),
        name="relay",
    )(route_code, incoming, second)

    bed, row, column = pl.pallas_call(
        bed_second_kernel,
        in_specs=[whole(SMEM), whole(), whole(), whole()],
        out_specs=[whole(), whole(), whole()],
        out_shape=[bed_type, in_vmem(runs), in_vmem(runs)],
        scratch_shapes=[in_vmem(runs), in_vmem(runs)] + bed_scratch,
        compiler_params=params(),
        cost_estimate=pl.CostEstimate(flops=10**9, bytes_accessed=10**7, transcendentals=0),
        name="bed_second",
    )(block_tile, bed_cell, incoming, bed)

    incoming = exchange(outgoing)

    final_mass, own, peer = pl.pallas_call(
        bed_third_kernel,
        in_specs=[whole()] * 4,
        out_specs=[whole(), whole(), whole()],
        out_shape=[
            jax.ShapeDtypeStruct((2 * NB, 128), jnp.float32),
            jax.ShapeDtypeStruct((4, 128), jnp.float32),
            jax.ShapeDtypeStruct((4, 128), jnp.float32),
        ],
        scratch_shapes=bed_scratch,
        compiler_params=params(),
        name="bed_third",
    )(row, column, incoming, bed)
    other = lax.ppermute(peer, "arch", swap)

    final_position = pl.pallas_call(
        finish_kernel,
        in_specs=[whole(), whole()],
        out_specs=whole(),
        out_shape=jax.ShapeDtypeStruct((3, PARTS), jnp.float32),
        compiler_params=params(),
        cost_estimate=pl.CostEstimate(flops=10**7, bytes_accessed=10**6, transcendentals=0),
        name="finish",
    )(incoming, third)
    return (
        final_position,
        final_mass.reshape(PARTS),
        (own + other).reshape(1, BEDC),
    )


def solution(mesh):
    one = P(("arch", "dom"))
    two = P(None, ("arch", "dom"))
    rows = P(None, ("arch", "dom"), None)
    return jax.shard_map(
        body,
        mesh=mesh,
        in_specs=(
            two, one, one, P(None, None, ("arch", "dom")),
            P(None, None, ("arch", "dom"), None), rows, rows, two, two, rows,
        ),
        out_specs=(two, one, P(("arch", "dom"), None)),
        check_vma=False,
    )
```

```python
import jax
import jax.numpy as jnp
from jax import lax
from jax.experimental import pallas as pl
from jax.experimental.pallas import tpu as pltpu
from jax.sharding import PartitionSpec as P

NB = 128
WIDTH = 256
PARTS = NB * WIDTH
CELLS = 2048
ROWS = CELLS // 128
BEDC = 512
TILES = 128
DT = 0.5
CHUNK = 32
GROUP = 32
SPAN = 64
LATER_UNROLL = 16

LINES = 6
FIRST_CODE = (16.0, 2.0**16)
SECOND_CODE = (24.0, 43690.0)
MASS_SCALE = 32767.0
FRAC_SCALE = 166000.0

VMEM = pltpu.VMEM
SMEM = pltpu.SMEM


def whole(space=VMEM):
    return pl.BlockSpec(memory_space=space)


def params(mebibytes=24):
    return pltpu.CompilerParams(vmem_limit_bytes=mebibytes * 1024 * 1024)


def in_hbm(*arrays):
    return [pltpu.with_memory_space_constraint(a, pltpu.HBM) for a in arrays]


def in_vmem(kind):
    return pltpu.VMEM(kind.shape, kind.dtype)


def sublane():
    return lax.broadcasted_iota(jnp.int32, (8, 128), 0)


def fill_table(table, vel, dif, step):
    for c in range(4):
        v = (vel[c] if c < 3 else dif[...]).astype(jnp.float32)
        total = v[step : step + 1] + v[step + 1 : step + 2]
        value = 0.5 * DT * total if c < 3 else jnp.sqrt(DT * total)
        for r in range(ROWS):
            row = value[:, 128 * r : 128 * (r + 1)]
            for at in (c, c + 3) if c < 3 else (6, 7):
                table[r, at : at + 1, :] = row


def halves(low, high, sub):
    of_low = (sub < 3) | (sub == 6)
    return jnp.where(of_low, jnp.broadcast_to(low, (8, 128)), jnp.broadcast_to(high, (8, 128)))


def stack_halves(ref, lead, start):
    low = ref[lead + (slice(None), pl.ds(start, 128))]
    high = ref[lead + (slice(None), pl.ds(start + 128, 128))]
    return jnp.concatenate([low, high, jnp.zeros((2, 128), jnp.float32)], axis=0)


def is_z(sub):
    return (sub == 2) | (sub == 5)


def encode(here, state, code, sub):
    offset, scale = code
    scales = jnp.where(is_z(sub), 2.0 * scale, scale)
    number = (here * scales + (offset * scales + 0.5)).astype(jnp.int32)
    upper = pltpu.roll(number, 6, 0) >> 11
    lower = pltpu.roll(number, 7, 0) & 2047
    word = (number << 11) | jnp.where((sub == 0) | (sub == 3), upper, lower)
    return jnp.where(is_z(sub), state, word)


def load_block(ref, j):
    rows = ref[pl.ds(LINES * j, LINES), :]
    return jnp.concatenate([rows, jnp.zeros((2, 128), jnp.int32)], axis=0)


def decode_position(word, code, sub):
    offset, scale = code
    shares = word & 2047
    z = (pltpu.roll(shares, 2, 0) << 11) | pltpu.roll(shares, 1, 0)
    number = jnp.where(is_z(sub), z, (word >> 11) & (2**21 - 1))
    return number.astype(jnp.float32) * jnp.where(is_z(sub), 0.5 / scale, 1.0 / scale) - offset


def advance(tables, slot, tile, index, noise, sub):
    lane = index & 127
    values = [
        jnp.take_along_axis(tables[slot, tile, r], lane, axis=1, mode="promise_in_bounds")
        for r in range(ROWS)
    ]
    bit = 128
    while len(values) > 1:
        odd = (index & bit) != 0
        values = [jnp.where(odd, b, a) for a, b in zip(values[0::2], values[1::2])]
        bit *= 2
    value = values[0]
    spread = jnp.take_along_axis(
        value, jnp.where(sub < 3, 6, 7), axis=0, mode="promise_in_bounds"
    )
    return value + spread * noise


def cells_of(cell_ref, step, start, sub):
    low = cell_ref[step : step + 1, pl.ds(start, 128)]
    high = cell_ref[step : step + 1, pl.ds(start + 128, 128)]
    return halves(low, high, sub)


def fraction(settling):
    return 1.0 - jnp.exp(-DT * settling)


def invert(route_ref, step, source_ref):
    def one(j, carry):
        source_ref[0, route_ref[step, 0, j]] = j
        return carry

    lax.fori_loop(0, NB, one, 0, unroll=16)


def load_kernel(
    route_in, tile_in, vel_in, dif_in, pos_in, mass_in, settle_in, noise_in, cell_in,
    pos_out, settle_out, noise_out, cell_out, code_ref, table_ref, tile_out, source_ref,
    mass_ref, vel_ref, dif_ref, route_ref, sems,
):
    pairs = [
        (route_in, route_ref), (tile_in, tile_out), (mass_in, mass_ref), (settle_in, settle_out),
        (vel_in, vel_ref), (dif_in, dif_ref), (cell_in, cell_out), (pos_in, pos_out),
        (noise_in.at[0], noise_out),
    ]
    copies = [pltpu.make_async_copy(a, b, sems.at[i]) for i, (a, b) in enumerate(pairs)]
    for copy in copies:
        copy.start()
    for copy in copies[2:4]:
        copy.wait()
    mass_code = (mass_ref[...] * MASS_SCALE + 0.5).astype(jnp.int32)
    mass_code = jnp.clip(mass_code, 0, 65535) - 32768
    frac_code = (fraction(settle_out[...]) * FRAC_SCALE + 0.5).astype(jnp.int32)
    frac_code = jnp.clip(frac_code, 0, 65535)
    code_ref[...] = mass_code * 65536 + frac_code
    for copy in copies[4:6]:
        copy.wait()
    fill_table(table_ref, vel_ref, dif_ref, 0)
    copies[0].wait()
    invert(route_ref, 0, source_ref)
    for copy in copies[1:2] + copies[6:]:
        copy.wait()


def send_chunks(block, rows_ref, out_ref, sems):
    span = LINES * CHUNK
    copies = []
    for part in range(NB // CHUNK):

        def one(k, carry, part=part):
            rows_ref[pl.ds(part * span + LINES * k, LINES), :] = block(part * CHUNK + k)
            return carry

        lax.fori_loop(0, CHUNK, one, 0, unroll=CHUNK)
        rows = pl.ds(part * span, span)
        copies.append(pltpu.make_async_copy(rows_ref.at[rows], out_ref.at[rows], sems.at[part]))
        copies[-1].start()
    for copy in copies:
        copy.wait()


def first_kernel(
    tile_ref, source_ref, peer_vel, peer_dif,
    pos_ref, settle_ref, noise_ref, cell_ref, code_ref, table_ref, out_ref, tables, rows_ref, sems,
):
    arch = lax.axis_index("arch")
    tables[0, arch] = table_ref[...]
    fill_table(tables.at[0, 1 - arch], peer_vel, peer_dif, 0)
    sub = sublane()
    fall = jnp.where(is_z(sub), -3.0 * DT, 0.0)

    def block(place):
        j = source_ref[0, place]
        start = pl.multiple_of(j * WIDTH, WIDTH)
        index = cells_of(cell_ref, 0, start, sub)
        noise = stack_halves(noise_ref, (), start)
        here = stack_halves(pos_ref, (), start)
        speed = halves(settle_ref[pl.ds(2 * j, 1), :], settle_ref[pl.ds(2 * j + 1, 1), :], sub)
        here = here + fall * speed
        here = here + advance(tables, 0, tile_ref[0, 0, j] // TILES, index, noise, sub)
        state = halves(code_ref[pl.ds(2 * j, 1), :], code_ref[pl.ds(2 * j + 1, 1), :], sub)
        return encode(here, state, FIRST_CODE, sub)[0:LINES]

    send_chunks(block, rows_ref, out_ref, sems)


def later_kernel(
    tile_ref, route_ref, own_vel, peer_vel, own_dif, peer_dif, noise_ref, cell_ref,
    second_ref, third_ref, source_ref, tables,
):
    arch = lax.axis_index("arch")
    part = pl.program_id(0)

    @pl.when(part == 0)
    def _():
        invert(route_ref, 1, source_ref)
        for step in (1, 2):
            fill_table(tables.at[step - 1, arch], own_vel, own_dif, step)
            fill_table(tables.at[step - 1, 1 - arch], peer_vel, peer_dif, step)

    sub = sublane()

    def block(j, carry):
        start = pl.multiple_of(j * WIDTH, WIDTH)
        slot = part * SPAN + j
        for step in (1, 2):
            index = cells_of(cell_ref, step, start, sub)
            noise = stack_halves(noise_ref, (step,), start)
            out_ref = second_ref if step == 1 else third_ref
            out_ref[j] = advance(
                tables, step - 1, tile_ref[step, 0, slot] // TILES, index, noise, sub
            )
        return carry

    lax.fori_loop(0, SPAN, block, 0, unroll=LATER_UNROLL)


def relay_kernel(source_ref, in_ref, add_ref, out_ref, rows_ref, sems):
    sub = sublane()

    def block(place):
        j = source_ref[0, place]
        word = load_block(in_ref, j)
        here = decode_position(word, FIRST_CODE, sub) + add_ref[j]
        return encode(here, word, SECOND_CODE, sub)[0:LINES]

    send_chunks(block, rows_ref, out_ref, sems)


def decode(code):
    mass = ((code >> 16) + 32768).astype(jnp.float32) * (1.0 / MASS_SCALE)
    frac = (code & 65535).astype(jnp.float32) * (1.0 / FRAC_SCALE)
    return mass, frac


def split_cells(tile_ref, bed_ref, step, row_ref, column_ref):
    def block(slot, carry):
        tile = tile_ref[step, 0, slot] // TILES
        for half in range(2):
            start = pl.multiple_of(slot * WIDTH + half * 128, 128)
            cell = bed_ref[step : step + 1, pl.ds(start, 128)]
            run = pl.ds(2 * slot + half, 1)
            row_ref[run, :] = ((cell >> 6) + tile * 8).astype(jnp.float32)
            column_ref[run, :] = (cell & 63).astype(jnp.float32)
        return carry

    lax.fori_loop(0, NB, block, 0, unroll=16)


def spread_run(ref, run):
    row = jnp.broadcast_to(ref[pl.ds(run, 1), :], (8, 128))
    return jnp.concatenate([row, row], axis=0).astype(jnp.bfloat16)


def histogram(row_ref, column_ref, dep, high_ref, rest_ref, lay_ref):
    high = dep.astype(jnp.bfloat16).astype(jnp.float32)
    high_ref[...] = high
    rest_ref[...] = dep - high
    places = lax.broadcasted_iota(jnp.int32, (64, 128), 0).astype(jnp.float32).astype(jnp.bfloat16)
    one, zero = jnp.bfloat16(1), jnp.bfloat16(0)

    def group(i, total):
        hits = []
        weights = []
        for k in range(2 * GROUP):
            run = 2 * GROUP * i + k
            mine = spread_run(row_ref, run) == places[0:16]
            parts = [jnp.where(mine, spread_run(ref, run), zero) for ref in (high_ref, rest_ref)]
            weights.append(jnp.concatenate(parts, axis=0))
            column = jnp.concatenate([spread_run(column_ref, run)] * 4, axis=0)
            hits.append(jnp.where(column == places, one, zero))
        weight = jnp.concatenate(weights, axis=1)
        hit = jnp.concatenate(hits, axis=1)
        return total + lax.dot_general(
            weight, hit, (((1,), (1,)), ((), ())), preferred_element_type=jnp.float32
        )

    total = lax.fori_loop(0, NB // GROUP, group, jnp.zeros((32, 64), jnp.float32), unroll=4)
    lay_ref[:, 0:64] = total[0:16] + total[16:32]
    return jnp.concatenate([lay_ref[pl.ds(i, 8, stride=2), 0:64] for i in range(2)], axis=1)


def bed_first_kernel(
    tile_ref, bed_ref, mass_ref, settle_ref, out_ref, row_ref, column_ref, *scratch
):
    split_cells(tile_ref, bed_ref, 0, row_ref, column_ref)
    dep = mass_ref[...] * fraction(settle_ref[...])
    out_ref[...] = histogram(row_ref, column_ref, dep, *scratch)


def bed_second_kernel(
    tile_ref, bed_ref, state_ref, before_ref, out_ref, next_row_ref, next_column_ref,
    row_ref, column_ref, *scratch,
):
    split_cells(tile_ref, bed_ref, 1, row_ref, column_ref)
    split_cells(tile_ref, bed_ref, 2, next_row_ref, next_column_ref)
    mass, frac = decode(state_ref[pl.ds(2, 2 * NB, stride=3), :])
    dep = mass * (1.0 - frac) * frac
    out_ref[...] = before_ref[...] + histogram(row_ref, column_ref, dep, *scratch)


def bed_third_kernel(
    row_ref, column_ref, state_ref, before_ref, mass_ref, own_ref, peer_ref, *scratch
):
    mass, frac = decode(state_ref[pl.ds(2, 2 * NB, stride=3), :])
    left = mass * (1.0 - frac) * (1.0 - frac)
    mass_ref[...] = left * (1.0 - frac)
    total = before_ref[...] + histogram(row_ref, column_ref, left * frac, *scratch)
    total = total * (BEDC / PARTS)
    first = lax.axis_index("arch") == 0
    own_ref[...] = jnp.where(first, total[0:4], total[4:8])
    peer_ref[...] = jnp.where(first, total[4:8], total[0:4])


def finish_kernel(in_ref, add_ref, out_ref):
    sub = sublane()

    def block(j, carry):
        start = pl.multiple_of(j * WIDTH, WIDTH)
        here = decode_position(load_block(in_ref, j), SECOND_CODE, sub) + add_ref[j]
        out_ref[:, pl.ds(start, 128)] = here[0:3]
        out_ref[:, pl.ds(start + 128, 128)] = here[3:6]
        return carry

    lax.fori_loop(0, NB, block, 0, unroll=16)


def exchange(outgoing):
    blocks = outgoing.reshape(NB, 1, LINES * 128)
    return lax.all_to_all(blocks, "dom", 0, 0, tiled=True).reshape(LINES * NB, 128)


def body(
    position, particle_mass, settling, walk_noise, velocity, diffusivity,
    block_tile, cell_index, bed_cell, route_code,
):
    slabs = velocity.shape[0]
    swap = [(0, 1), (1, 0)]
    vel = velocity.transpose(1, 2, 0, 3).reshape(3, slabs, CELLS)
    dif = diffusivity.transpose(1, 0, 2).reshape(slabs, CELLS)
    peer_vel = lax.ppermute(vel, "arch", swap)
    peer_dif = lax.ppermute(dif, "arch", swap)
    mass = particle_mass.reshape(2 * NB, 128)
    settle = settling.reshape(2 * NB, 128)

    state_type = jax.ShapeDtypeStruct((LINES * NB, 128), jnp.int32)
    move_type = jax.ShapeDtypeStruct((NB, 8, 128), jnp.float32)
    bed_type = jax.ShapeDtypeStruct((8, 128), jnp.float32)
    steps = NB // SPAN
    span = SPAN * WIDTH
    runs = jax.ShapeDtypeStruct((2 * NB, 128), jnp.float32)
    bed_scratch = [in_vmem(runs), in_vmem(runs), pltpu.VMEM((16, 128), jnp.float32)]

    *loaded, tiles, sources = pl.pallas_call(
        load_kernel,
        in_specs=[whole(pl.ANY)] * 9,
        out_specs=[whole()] * 6 + [whole(SMEM)] * 2,
        out_shape=[
            pltpu.VMEM((3, PARTS), jnp.float32),
            in_vmem(runs),
            pltpu.VMEM((3, PARTS), jnp.float32),
            pltpu.VMEM((3, PARTS), jnp.int32),
            pltpu.VMEM((2 * NB, 128), jnp.int32),
            pltpu.VMEM((ROWS, 8, 128), jnp.float32),
            pltpu.SMEM(block_tile.shape, jnp.int32),
            pltpu.SMEM((1, NB), jnp.int32),
        ],
        scratch_shapes=[
            in_vmem(runs), in_vmem(vel), in_vmem(dif),
            pltpu.SMEM(route_code.shape, jnp.int32), pltpu.SemaphoreType.DMA((9,)),
        ],
        compiler_params=params(),
        cost_estimate=pl.CostEstimate(flops=10**7, bytes_accessed=4 * 10**6, transcendentals=0),
        name="load",
    )(
        *in_hbm(route_code, block_tile, vel, dif),
        *in_hbm(position, mass, settle, walk_noise, cell_index),
    )

    send_scratch = [
        pltpu.VMEM((LINES * NB, 128), jnp.int32), pltpu.SemaphoreType.DMA((NB // CHUNK,)),
    ]
    outgoing = pl.pallas_call(
        first_kernel,
        in_specs=[whole(SMEM), whole(SMEM)] + [whole()] * 8,
        out_specs=whole(pltpu.HBM),
        out_shape=state_type,
        scratch_shapes=[pltpu.VMEM((1, 2, ROWS, 8, 128), jnp.float32)] + send_scratch,
        compiler_params=params(),
        name="first",
    )(tiles, sources, peer_vel, peer_dif, *loaded)

    incoming = exchange(outgoing)

    second, third, later_sources = pl.pallas_call(
        later_kernel,
        grid=(steps,),
        in_specs=[whole(SMEM), whole(SMEM), whole(), whole(), whole(), whole()]
        + [
            pl.BlockSpec((3, 3, span), lambda i: (0, 0, i)),
            pl.BlockSpec((3, span), lambda i: (0, i)),
        ],
        out_specs=[pl.BlockSpec((SPAN, 8, 128), lambda i: (i, 0, 0))] * 2 + [whole(SMEM)],
        out_shape=[in_vmem(move_type), in_vmem(move_type), pltpu.SMEM((1, NB), jnp.int32)],
        scratch_shapes=[pltpu.VMEM((2, 2, ROWS, 8, 128), jnp.float32)],
        compiler_params=params(),
        cost_estimate=pl.CostEstimate(flops=10**9, bytes_accessed=10**7, transcendentals=0),
        name="later",
    )(*in_hbm(block_tile, route_code, vel), peer_vel, *in_hbm(dif), peer_dif, *in_hbm(walk_noise, cell_index))

    bed = pl.pallas_call(
        bed_first_kernel,
        in_specs=[whole(SMEM), whole(), whole(), whole()],
        out_specs=whole(),
        out_shape=bed_type,
        scratch_shapes=[in_vmem(runs), in_vmem(runs)] + bed_scratch,
        compiler_params=params(),
        cost_estimate=pl.CostEstimate(flops=10**9, bytes_accessed=10**7, transcendentals=0),
        name="bed_first",
    )(block_tile, bed_cell, mass, settle)

    outgoing = pl.pallas_call(
        relay_kernel,
        in_specs=[whole(SMEM), whole(), whole()],
        out_specs=whole(pltpu.HBM),
        out_shape=state_type,
        scratch_shapes=send_scratch,
        compiler_params=params(),
        name="relay",
    )(later_sources, incoming, second)

    bed, row, column = pl.pallas_call(
        bed_second_kernel,
        in_specs=[whole(SMEM), whole(), whole(), whole()],
        out_specs=[whole(), whole(), whole()],
        out_shape=[bed_type, in_vmem(runs), in_vmem(runs)],
        scratch_shapes=[in_vmem(runs), in_vmem(runs)] + bed_scratch,
        compiler_params=params(),
        cost_estimate=pl.CostEstimate(flops=10**9, bytes_accessed=10**7, transcendentals=0),
        name="bed_second",
    )(block_tile, bed_cell, incoming, bed)

    incoming = exchange(outgoing)

    final_mass, own, peer = pl.pallas_call(
        bed_third_kernel,
        in_specs=[whole()] * 4,
        out_specs=[whole(), whole(), whole()],
        out_shape=[
            jax.ShapeDtypeStruct((2 * NB, 128), jnp.float32),
            jax.ShapeDtypeStruct((4, 128), jnp.float32),
            jax.ShapeDtypeStruct((4, 128), jnp.float32),
        ],
        scratch_shapes=bed_scratch,
        compiler_params=params(),
        name="bed_third",
    )(row, column, incoming, bed)
    other = lax.ppermute(peer, "arch", swap)

    final_position = pl.pallas_call(
        finish_kernel,
        in_specs=[whole(), whole()],
        out_specs=whole(),
        out_shape=jax.ShapeDtypeStruct((3, PARTS), jnp.float32),
        compiler_params=params(),
        cost_estimate=pl.CostEstimate(flops=10**7, bytes_accessed=10**6, transcendentals=0),
        name="finish",
    )(incoming, third)
    return (
        final_position,
        final_mass.reshape(PARTS),
        (own + other).reshape(1, BEDC),
    )


def solution(mesh):
    one = P(("arch", "dom"))
    two = P(None, ("arch", "dom"))
    rows = P(None, ("arch", "dom"), None)
    return jax.shard_map(
        body,
        mesh=mesh,
        in_specs=(
            two, one, one, P(None, None, ("arch", "dom")),
            P(None, None, ("arch", "dom"), None), rows, rows, two, two, rows,
        ),
        out_specs=(two, one, P(("arch", "dom"), None)),
        check_vma=False,
    )
```

```python
import jax
import jax.numpy as jnp
from jax import lax
from jax.experimental import pallas as pl
from jax.experimental.pallas import tpu as pltpu
from jax.sharding import PartitionSpec as P

NB = 128
WIDTH = 256
PARTS = NB * WIDTH
CELLS = 2048
ROWS = CELLS // 128
BEDC = 512
TILES = 128
DT = 0.5
CHUNK = 32
GROUP = 32
SPAN = 64
LATER_UNROLL = 16

LINES = 6
FIRST_CODE = (16.0, 2.0**16)
SECOND_CODE = (24.0, 43690.0)
MASS_SCALE = 32767.0
FRAC_SCALE = 166000.0

VMEM = pltpu.VMEM
SMEM = pltpu.SMEM


def whole(space=VMEM):
    return pl.BlockSpec(memory_space=space)


def params(mebibytes=24):
    return pltpu.CompilerParams(vmem_limit_bytes=mebibytes * 1024 * 1024)


def in_hbm(*arrays):
    return [pltpu.with_memory_space_constraint(a, pltpu.HBM) for a in arrays]


def in_vmem(kind):
    return pltpu.VMEM(kind.shape, kind.dtype)


def sublane():
    return lax.broadcasted_iota(jnp.int32, (8, 128), 0)


def fill_table(table, vel, dif, step):
    for c in range(4):
        v = (vel[c] if c < 3 else dif[...]).astype(jnp.float32)
        total = v[step : step + 1] + v[step + 1 : step + 2]
        value = 0.5 * DT * total if c < 3 else jnp.sqrt(DT * total)
        for r in range(ROWS):
            row = value[:, 128 * r : 128 * (r + 1)]
            for at in (c, c + 3) if c < 3 else (6, 7):
                table[r, at : at + 1, :] = row


def halves(low, high, sub):
    of_low = (sub < 3) | (sub == 6)
    return jnp.where(of_low, jnp.broadcast_to(low, (8, 128)), jnp.broadcast_to(high, (8, 128)))


def stack_halves(ref, lead, start):
    low = ref[lead + (slice(None), pl.ds(start, 128))]
    high = ref[lead + (slice(None), pl.ds(start + 128, 128))]
    return jnp.concatenate([low, high, jnp.zeros((2, 128), jnp.float32)], axis=0)


def is_z(sub):
    return (sub == 2) | (sub == 5)


def encode(here, state, code, sub):
    offset, scale = code
    scales = jnp.where(is_z(sub), 2.0 * scale, scale)
    number = (here * scales + (offset * scales + 0.5)).astype(jnp.int32)
    upper = pltpu.roll(number, 6, 0) >> 11
    lower = pltpu.roll(number, 7, 0) & 2047
    word = (number << 11) | jnp.where((sub == 0) | (sub == 3), upper, lower)
    return jnp.where(is_z(sub), state, word)


def load_block(ref, j):
    rows = ref[pl.ds(LINES * j, LINES), :]
    return jnp.concatenate([rows, jnp.zeros((2, 128), jnp.int32)], axis=0)


def decode_position(word, code, sub):
    offset, scale = code
    shares = word & 2047
    z = (pltpu.roll(shares, 2, 0) << 11) | pltpu.roll(shares, 1, 0)
    number = jnp.where(is_z(sub), z, (word >> 11) & (2**21 - 1))
    return number.astype(jnp.float32) * jnp.where(is_z(sub), 0.5 / scale, 1.0 / scale) - offset


def advance(tables, slot, tile, index, noise, sub):
    lane = index & 127
    values = [
        jnp.take_along_axis(tables[slot, tile, r], lane, axis=1, mode="promise_in_bounds")
        for r in range(ROWS)
    ]
    bit = 128
    while len(values) > 1:
        odd = (index & bit) != 0
        values = [jnp.where(odd, b, a) for a, b in zip(values[0::2], values[1::2])]
        bit *= 2
    value = values[0]
    spread = jnp.take_along_axis(
        value, jnp.where(sub < 3, 6, 7), axis=0, mode="promise_in_bounds"
    )
    return value + spread * noise


def cells_of(cell_ref, step, start, sub):
    low = cell_ref[step : step + 1, pl.ds(start, 128)]
    high = cell_ref[step : step + 1, pl.ds(start + 128, 128)]
    return halves(low, high, sub)


def fraction(settling):
    return 1.0 - jnp.exp(-DT * settling)


def invert(route_ref, step, source_ref):
    def one(j, carry):
        source_ref[0, route_ref[step, 0, j]] = j
        return carry

    lax.fori_loop(0, NB, one, 0, unroll=16)


def load_kernel(
    route_in, tile_in, vel_in, dif_in, pos_in, mass_in, settle_in, noise_in, cell_in,
    pos_out, settle_out, noise_out, cell_out, code_ref, table_ref, tile_out, source_ref,
    mass_ref, vel_ref, dif_ref, route_ref, sems,
):
    pairs = [
        (route_in, route_ref), (tile_in, tile_out), (mass_in, mass_ref), (settle_in, settle_out),
        (vel_in, vel_ref), (dif_in, dif_ref), (cell_in, cell_out), (pos_in, pos_out),
        (noise_in.at[0], noise_out),
    ]
    copies = [pltpu.make_async_copy(a, b, sems.at[i]) for i, (a, b) in enumerate(pairs)]
    for copy in copies:
        copy.start()
    for copy in copies[2:4]:
        copy.wait()
    mass_code = (mass_ref[...] * MASS_SCALE + 0.5).astype(jnp.int32)
    mass_code = jnp.clip(mass_code, 0, 65535) - 32768
    frac_code = (fraction(settle_out[...]) * FRAC_SCALE + 0.5).astype(jnp.int32)
    frac_code = jnp.clip(frac_code, 0, 65535)
    code_ref[...] = mass_code * 65536 + frac_code
    for copy in copies[4:6]:
        copy.wait()
    fill_table(table_ref, vel_ref, dif_ref, 0)
    copies[0].wait()
    invert(route_ref, 0, source_ref)
    for copy in copies[1:2] + copies[6:]:
        copy.wait()


def send_chunks(block, rows_ref, out_ref, sems):
    span = LINES * CHUNK
    copies = []
    for part in range(NB // CHUNK):

        def one(k, carry, part=part):
            rows_ref[pl.ds(part * span + LINES * k, LINES), :] = block(part * CHUNK + k)
            return carry

        lax.fori_loop(0, CHUNK, one, 0, unroll=CHUNK)
        rows = pl.ds(part * span, span)
        copies.append(pltpu.make_async_copy(rows_ref.at[rows], out_ref.at[rows], sems.at[part]))
        copies[-1].start()
    for copy in copies:
        copy.wait()


def first_kernel(
    tile_ref, source_ref, peer_vel, peer_dif,
    pos_ref, settle_ref, noise_ref, cell_ref, code_ref, table_ref, out_ref, tables, rows_ref, sems,
):
    arch = lax.axis_index("arch")
    tables[0, arch] = table_ref[...]
    fill_table(tables.at[0, 1 - arch], peer_vel, peer_dif, 0)
    sub = sublane()
    fall = jnp.where(is_z(sub), -3.0 * DT, 0.0)

    def block(place):
        j = source_ref[0, place]
        start = pl.multiple_of(j * WIDTH, WIDTH)
        index = cells_of(cell_ref, 0, start, sub)
        noise = stack_halves(noise_ref, (), start)
        here = stack_halves(pos_ref, (), start)
        speed = halves(settle_ref[pl.ds(2 * j, 1), :], settle_ref[pl.ds(2 * j + 1, 1), :], sub)
        here = here + fall * speed
        here = here + advance(tables, 0, tile_ref[0, 0, j] // TILES, index, noise, sub)
        state = halves(code_ref[pl.ds(2 * j, 1), :], code_ref[pl.ds(2 * j + 1, 1), :], sub)
        return encode(here, state, FIRST_CODE, sub)[0:LINES]

    send_chunks(block, rows_ref, out_ref, sems)


def later_kernel(
    tile_ref, route_ref, own_vel, peer_vel, own_dif, peer_dif, noise_ref, cell_ref,
    second_ref, third_ref, source_ref, tables,
):
    arch = lax.axis_index("arch")
    part = pl.program_id(0)

    @pl.when(part == 0)
    def _():
        invert(route_ref, 1, source_ref)
        for step in (1, 2):
            fill_table(tables.at[step - 1, arch], own_vel, own_dif, step)
            fill_table(tables.at[step - 1, 1 - arch], peer_vel, peer_dif, step)

    sub = sublane()

    def block(j, carry):
        start = pl.multiple_of(j * WIDTH, WIDTH)
        slot = part * SPAN + j
        for step in (1, 2):
            index = cells_of(cell_ref, step, start, sub)
            noise = stack_halves(noise_ref, (step,), start)
            out_ref = second_ref if step == 1 else third_ref
            out_ref[j] = advance(
                tables, step - 1, tile_ref[step, 0, slot] // TILES, index, noise, sub
            )
        return carry

    lax.fori_loop(0, SPAN, block, 0, unroll=LATER_UNROLL)


def relay_kernel(source_ref, in_ref, add_ref, out_ref, rows_ref, sems):
    sub = sublane()

    def block(place):
        j = source_ref[0, place]
        word = load_block(in_ref, j)
        here = decode_position(word, FIRST_CODE, sub) + add_ref[j]
        return encode(here, word, SECOND_CODE, sub)[0:LINES]

    send_chunks(block, rows_ref, out_ref, sems)


def decode(code):
    mass = ((code >> 16) + 32768).astype(jnp.float32) * (1.0 / MASS_SCALE)
    frac = (code & 65535).astype(jnp.float32) * (1.0 / FRAC_SCALE)
    return mass, frac


def split_cells(tile_ref, bed_ref, step, row_ref, column_ref):
    def block(slot, carry):
        tile = tile_ref[step, 0, slot] // TILES
        for half in range(2):
            start = pl.multiple_of(slot * WIDTH + half * 128, 128)
            cell = bed_ref[step : step + 1, pl.ds(start, 128)]
            run = pl.ds(2 * slot + half, 1)
            row_ref[run, :] = ((cell >> 6) + tile * 8).astype(jnp.float32)
            column_ref[run, :] = (cell & 63).astype(jnp.float32)
        return carry

    lax.fori_loop(0, NB, block, 0, unroll=16)


def spread_run(ref, run):
    row = jnp.broadcast_to(ref[pl.ds(run, 1), :], (8, 128))
    return jnp.concatenate([row, row], axis=0).astype(jnp.bfloat16)


def histogram(row_ref, column_ref, dep, high_ref, rest_ref, lay_ref):
    high = dep.astype(jnp.bfloat16).astype(jnp.float32)
    high_ref[...] = high
    rest_ref[...] = dep - high
    places = lax.broadcasted_iota(jnp.int32, (64, 128), 0).astype(jnp.float32).astype(jnp.bfloat16)
    one, zero = jnp.bfloat16(1), jnp.bfloat16(0)

    def group(i, total):
        hits = []
        weights = []
        for k in range(2 * GROUP):
            run = 2 * GROUP * i + k
            mine = spread_run(row_ref, run) == places[0:16]
            parts = [jnp.where(mine, spread_run(ref, run), zero) for ref in (high_ref, rest_ref)]
            weights.append(jnp.concatenate(parts, axis=0))
            column = jnp.concatenate([spread_run(column_ref, run)] * 4, axis=0)
            hits.append(jnp.where(column == places, one, zero))
        weight = jnp.concatenate(weights, axis=1)
        hit = jnp.concatenate(hits, axis=1)
        return total + lax.dot_general(
            weight, hit, (((1,), (1,)), ((), ())), preferred_element_type=jnp.float32
        )

    total = lax.fori_loop(0, NB // GROUP, group, jnp.zeros((32, 64), jnp.float32), unroll=4)
    lay_ref[:, 0:64] = total[0:16] + total[16:32]
    return jnp.concatenate([lay_ref[pl.ds(i, 8, stride=2), 0:64] for i in range(2)], axis=1)


def bed_first_kernel(
    tile_ref, bed_ref, mass_ref, settle_ref, out_ref, row_ref, column_ref, *scratch
):
    split_cells(tile_ref, bed_ref, 0, row_ref, column_ref)
    dep = mass_ref[...] * fraction(settle_ref[...])
    out_ref[...] = histogram(row_ref, column_ref, dep, *scratch)


def bed_second_kernel(
    tile_ref, bed_ref, state_ref, before_ref, out_ref, next_row_ref, next_column_ref,
    row_ref, column_ref, *scratch,
):
    split_cells(tile_ref, bed_ref, 1, row_ref, column_ref)
    split_cells(tile_ref, bed_ref, 2, next_row_ref, next_column_ref)
    mass, frac = decode(state_ref[pl.ds(2, 2 * NB, stride=3), :])
    dep = mass * (1.0 - frac) * frac
    out_ref[...] = before_ref[...] + histogram(row_ref, column_ref, dep, *scratch)


def bed_third_kernel(
    row_ref, column_ref, state_ref, before_ref, own_ref, peer_ref, *scratch
):
    mass, frac = decode(state_ref[pl.ds(2, 2 * NB, stride=3), :])
    dep = mass * (1.0 - frac) * (1.0 - frac) * frac
    total = before_ref[...] + histogram(row_ref, column_ref, dep, *scratch)
    total = total * (BEDC / PARTS)
    first = lax.axis_index("arch") == 0
    own_ref[...] = jnp.where(first, total[0:4], total[4:8])
    peer_ref[...] = jnp.where(first, total[4:8], total[0:4])


def finish_kernel(in_ref, add_ref, out_ref, mass_out, rows_ref, mass_ref, sems):
    sub = sublane()
    mass, frac = decode(in_ref[pl.ds(2, 2 * NB, stride=3), :])
    mass_ref[...] = mass * (1.0 - frac) * (1.0 - frac) * (1.0 - frac)
    copies = [pltpu.make_async_copy(mass_ref, mass_out, sems.at[NB // CHUNK])]
    copies[0].start()
    for part in range(NB // CHUNK):

        def block(k, carry, part=part):
            j = part * CHUNK + k
            start = pl.multiple_of(j * WIDTH, WIDTH)
            here = decode_position(load_block(in_ref, j), SECOND_CODE, sub) + add_ref[j]
            rows_ref[:, pl.ds(start, 128)] = here[0:3]
            rows_ref[:, pl.ds(start + 128, 128)] = here[3:6]
            return carry

        lax.fori_loop(0, CHUNK, block, 0, unroll=16)
        span = pl.ds(part * CHUNK * WIDTH, CHUNK * WIDTH)
        copies.append(
            pltpu.make_async_copy(rows_ref.at[:, span], out_ref.at[:, span], sems.at[part])
        )
        copies[-1].start()
    for copy in copies:
        copy.wait()


def exchange(outgoing):
    blocks = outgoing.reshape(NB, 1, LINES * 128)
    return lax.all_to_all(blocks, "dom", 0, 0, tiled=True).reshape(LINES * NB, 128)


def body(
    position, particle_mass, settling, walk_noise, velocity, diffusivity,
    block_tile, cell_index, bed_cell, route_code,
):
    slabs = velocity.shape[0]
    swap = [(0, 1), (1, 0)]
    vel = velocity.transpose(1, 2, 0, 3).reshape(3, slabs, CELLS)
    dif = diffusivity.transpose(1, 0, 2).reshape(slabs, CELLS)
    peer_vel = lax.ppermute(vel, "arch", swap)
    peer_dif = lax.ppermute(dif, "arch", swap)
    mass = particle_mass.reshape(2 * NB, 128)
    settle = settling.reshape(2 * NB, 128)

    state_type = jax.ShapeDtypeStruct((LINES * NB, 128), jnp.int32)
    move_type = jax.ShapeDtypeStruct((NB, 8, 128), jnp.float32)
    bed_type = jax.ShapeDtypeStruct((8, 128), jnp.float32)
    steps = NB // SPAN
    span = SPAN * WIDTH
    runs = jax.ShapeDtypeStruct((2 * NB, 128), jnp.float32)
    bed_scratch = [in_vmem(runs), in_vmem(runs), pltpu.VMEM((16, 128), jnp.float32)]

    *loaded, tiles, sources = pl.pallas_call(
        load_kernel,
        in_specs=[whole(pl.ANY)] * 9,
        out_specs=[whole()] * 6 + [whole(SMEM)] * 2,
        out_shape=[
            pltpu.VMEM((3, PARTS), jnp.float32),
            in_vmem(runs),
            pltpu.VMEM((3, PARTS), jnp.float32),
            pltpu.VMEM((3, PARTS), jnp.int32),
            pltpu.VMEM((2 * NB, 128), jnp.int32),
            pltpu.VMEM((ROWS, 8, 128), jnp.float32),
            pltpu.SMEM(block_tile.shape, jnp.int32),
            pltpu.SMEM((1, NB), jnp.int32),
        ],
        scratch_shapes=[
            in_vmem(runs), in_vmem(vel), in_vmem(dif),
            pltpu.SMEM(route_code.shape, jnp.int32), pltpu.SemaphoreType.DMA((9,)),
        ],
        compiler_params=params(),
        cost_estimate=pl.CostEstimate(flops=10**7, bytes_accessed=4 * 10**6, transcendentals=0),
        name="load",
    )(
        *in_hbm(route_code, block_tile, vel, dif),
        *in_hbm(position, mass, settle, walk_noise, cell_index),
    )

    send_scratch = [
        pltpu.VMEM((LINES * NB, 128), jnp.int32), pltpu.SemaphoreType.DMA((NB // CHUNK,)),
    ]
    outgoing = pl.pallas_call(
        first_kernel,
        in_specs=[whole(SMEM), whole(SMEM)] + [whole()] * 8,
        out_specs=whole(pltpu.HBM),
        out_shape=state_type,
        scratch_shapes=[pltpu.VMEM((1, 2, ROWS, 8, 128), jnp.float32)] + send_scratch,
        compiler_params=params(),
        name="first",
    )(tiles, sources, peer_vel, peer_dif, *loaded)

    incoming = exchange(outgoing)

    second, third, later_sources = pl.pallas_call(
        later_kernel,
        grid=(steps,),
        in_specs=[whole(SMEM), whole(SMEM), whole(), whole(), whole(), whole()]
        + [
            pl.BlockSpec((3, 3, span), lambda i: (0, 0, i)),
            pl.BlockSpec((3, span), lambda i: (0, i)),
        ],
        out_specs=[pl.BlockSpec((SPAN, 8, 128), lambda i: (i, 0, 0))] * 2 + [whole(SMEM)],
        out_shape=[in_vmem(move_type), in_vmem(move_type), pltpu.SMEM((1, NB), jnp.int32)],
        scratch_shapes=[pltpu.VMEM((2, 2, ROWS, 8, 128), jnp.float32)],
        compiler_params=params(),
        cost_estimate=pl.CostEstimate(flops=10**9, bytes_accessed=10**7, transcendentals=0),
        name="later",
    )(*in_hbm(block_tile, route_code, vel), peer_vel, *in_hbm(dif), peer_dif, *in_hbm(walk_noise, cell_index))

    bed = pl.pallas_call(
        bed_first_kernel,
        in_specs=[whole(SMEM), whole(), whole(), whole()],
        out_specs=whole(),
        out_shape=bed_type,
        scratch_shapes=[in_vmem(runs), in_vmem(runs)] + bed_scratch,
        compiler_params=params(),
        cost_estimate=pl.CostEstimate(flops=10**9, bytes_accessed=10**7, transcendentals=0),
        name="bed_first",
    )(block_tile, bed_cell, mass, settle)

    outgoing = pl.pallas_call(
        relay_kernel,
        in_specs=[whole(SMEM), whole(), whole()],
        out_specs=whole(pltpu.HBM),
        out_shape=state_type,
        scratch_shapes=send_scratch,
        compiler_params=params(),
        name="relay",
    )(later_sources, incoming, second)

    bed, row, column = pl.pallas_call(
        bed_second_kernel,
        in_specs=[whole(SMEM), whole(), whole(), whole()],
        out_specs=[whole(), whole(), whole()],
        out_shape=[bed_type, in_vmem(runs), in_vmem(runs)],
        scratch_shapes=[in_vmem(runs), in_vmem(runs)] + bed_scratch,
        compiler_params=params(),
        cost_estimate=pl.CostEstimate(flops=10**9, bytes_accessed=10**7, transcendentals=0),
        name="bed_second",
    )(block_tile, bed_cell, incoming, bed)

    incoming = exchange(outgoing)

    own, peer = pl.pallas_call(
        bed_third_kernel,
        in_specs=[whole()] * 4,
        out_specs=[whole(), whole()],
        out_shape=[
            jax.ShapeDtypeStruct((4, 128), jnp.float32),
            jax.ShapeDtypeStruct((4, 128), jnp.float32),
        ],
        scratch_shapes=bed_scratch,
        compiler_params=params(),
        name="bed_third",
    )(row, column, incoming, bed)
    other = lax.ppermute(peer, "arch", swap)

    final_position, final_mass = pl.pallas_call(
        finish_kernel,
        in_specs=[whole(), whole()],
        out_specs=[whole(pltpu.HBM), whole(pltpu.HBM)],
        out_shape=[jax.ShapeDtypeStruct((3, PARTS), jnp.float32), runs],
        scratch_shapes=[
            pltpu.VMEM((3, PARTS), jnp.float32), in_vmem(runs),
            pltpu.SemaphoreType.DMA((NB // CHUNK + 1,)),
        ],
        compiler_params=params(),
        cost_estimate=pl.CostEstimate(flops=10**7, bytes_accessed=10**6, transcendentals=0),
        name="finish",
    )(incoming, third)
    return (
        final_position,
        final_mass.reshape(PARTS),
        (own + other).reshape(1, BEDC),
    )


def solution(mesh):
    one = P(("arch", "dom"))
    two = P(None, ("arch", "dom"))
    rows = P(None, ("arch", "dom"), None)
    return jax.shard_map(
        body,
        mesh=mesh,
        in_specs=(
            two, one, one, P(None, None, ("arch", "dom")),
            P(None, None, ("arch", "dom"), None), rows, rows, two, two, rows,
        ),
        out_specs=(two, one, P(("arch", "dom"), None)),
        check_vma=False,
    )
```

```python
import jax
import jax.numpy as jnp
from jax import lax
from jax.experimental import pallas as pl
from jax.experimental.pallas import tpu as pltpu
from jax.sharding import PartitionSpec as P

NB = 128
WIDTH = 256
PARTS = NB * WIDTH
CELLS = 2048
ROWS = CELLS // 128
BEDC = 512
TILES = 128
DT = 0.5
CHUNK = 32
GROUP = 32
SPAN = 64
LATER_UNROLL = 16

LINES = 6
FIRST_CODE = (16.0, 2.0**16)
SECOND_CODE = (24.0, 43690.0)
MASS_SCALE = 32767.0
FRAC_SCALE = 166000.0

VMEM = pltpu.VMEM
SMEM = pltpu.SMEM


def whole(space=VMEM):
    return pl.BlockSpec(memory_space=space)


def params(mebibytes=24):
    return pltpu.CompilerParams(vmem_limit_bytes=mebibytes * 1024 * 1024)


def in_hbm(*arrays):
    return [pltpu.with_memory_space_constraint(a, pltpu.HBM) for a in arrays]


def in_vmem(kind):
    return pltpu.VMEM(kind.shape, kind.dtype)


def sublane():
    return lax.broadcasted_iota(jnp.int32, (8, 128), 0)


def fill_table(table, vel, dif, step):
    for c in range(4):
        v = (vel[c] if c < 3 else dif[...]).astype(jnp.float32)
        total = v[step : step + 1] + v[step + 1 : step + 2]
        value = 0.5 * DT * total if c < 3 else jnp.sqrt(DT * total)
        for r in range(ROWS):
            row = value[:, 128 * r : 128 * (r + 1)]
            for at in (c, c + 3) if c < 3 else (6, 7):
                table[r, at : at + 1, :] = row


def halves(low, high, sub):
    of_low = (sub < 3) | (sub == 6)
    return jnp.where(of_low, jnp.broadcast_to(low, (8, 128)), jnp.broadcast_to(high, (8, 128)))


def stack_halves(ref, lead, start):
    low = ref[lead + (slice(None), pl.ds(start, 128))]
    high = ref[lead + (slice(None), pl.ds(start + 128, 128))]
    return jnp.concatenate([low, high, jnp.zeros((2, 128), jnp.float32)], axis=0)


def is_z(sub):
    return (sub == 2) | (sub == 5)


def encode(here, state, code, sub):
    offset, scale = code
    scales = jnp.where(is_z(sub), 2.0 * scale, scale)
    number = (here * scales + (offset * scales + 0.5)).astype(jnp.int32)
    upper = pltpu.roll(number, 6, 0) >> 11
    lower = pltpu.roll(number, 7, 0) & 2047
    word = (number << 11) | jnp.where((sub == 0) | (sub == 3), upper, lower)
    return jnp.where(is_z(sub), state, word)


def load_block(ref, j):
    rows = ref[pl.ds(LINES * j, LINES), :]
    return jnp.concatenate([rows, jnp.zeros((2, 128), jnp.int32)], axis=0)


def decode_position(word, code, sub):
    offset, scale = code
    shares = word & 2047
    z = (pltpu.roll(shares, 2, 0) << 11) | pltpu.roll(shares, 1, 0)
    number = jnp.where(is_z(sub), z, (word >> 11) & (2**21 - 1))
    return number.astype(jnp.float32) * jnp.where(is_z(sub), 0.5 / scale, 1.0 / scale) - offset


def advance(tables, slot, tile, index, noise, sub):
    lane = index & 127
    values = [
        jnp.take_along_axis(tables[slot, tile, r], lane, axis=1, mode="promise_in_bounds")
        for r in range(ROWS)
    ]
    bit = 128
    while len(values) > 1:
        odd = (index & bit) != 0
        values = [jnp.where(odd, b, a) for a, b in zip(values[0::2], values[1::2])]
        bit *= 2
    value = values[0]
    spread = jnp.take_along_axis(
        value, jnp.where(sub < 3, 6, 7), axis=0, mode="promise_in_bounds"
    )
    return value + spread * noise


def cells_of(cell_ref, step, start, sub):
    low = cell_ref[step : step + 1, pl.ds(start, 128)]
    high = cell_ref[step : step + 1, pl.ds(start + 128, 128)]
    return halves(low, high, sub)


def fraction(settling):
    return 1.0 - jnp.exp(-DT * settling)


def invert(route_ref, step, source_ref):
    def one(j, carry):
        source_ref[0, route_ref[step, 0, j]] = j
        return carry

    lax.fori_loop(0, NB, one, 0, unroll=16)


def load_kernel(
    route_in, tile_in, vel_in, dif_in, pos_in, mass_in, settle_in, noise_in, cell_in,
    pos_out, settle_out, noise_out, cell_out, code_ref, table_ref, tile_out, source_ref,
    mass_ref, vel_ref, dif_ref, route_ref, sems,
):
    pairs = [
        (route_in, route_ref), (tile_in, tile_out), (mass_in, mass_ref), (settle_in, settle_out),
        (vel_in, vel_ref), (dif_in, dif_ref), (cell_in, cell_out), (pos_in, pos_out),
        (noise_in.at[0], noise_out),
    ]
    copies = [pltpu.make_async_copy(a, b, sems.at[i]) for i, (a, b) in enumerate(pairs)]
    for copy in copies:
        copy.start()
    for copy in copies[2:4]:
        copy.wait()
    mass_code = (mass_ref[...] * MASS_SCALE + 0.5).astype(jnp.int32)
    mass_code = jnp.clip(mass_code, 0, 65535) - 32768
    frac_code = (fraction(settle_out[...]) * FRAC_SCALE + 0.5).astype(jnp.int32)
    frac_code = jnp.clip(frac_code, 0, 65535)
    code_ref[...] = mass_code * 65536 + frac_code
    for copy in copies[4:6]:
        copy.wait()
    fill_table(table_ref, vel_ref, dif_ref, 0)
    copies[0].wait()
    invert(route_ref, 0, source_ref)
    for copy in copies[1:2] + copies[6:]:
        copy.wait()


def send_chunks(block, rows_ref, out_ref, sems):
    span = LINES * CHUNK
    copies = []
    for part in range(NB // CHUNK):

        def one(k, carry, part=part):
            rows_ref[pl.ds(part * span + LINES * k, LINES), :] = block(part * CHUNK + k)
            return carry

        lax.fori_loop(0, CHUNK, one, 0, unroll=CHUNK)
        rows = pl.ds(part * span, span)
        copies.append(pltpu.make_async_copy(rows_ref.at[rows], out_ref.at[rows], sems.at[part]))
        copies[-1].start()
    for copy in copies:
        copy.wait()


def first_kernel(
    tile_ref, source_ref, peer_vel, peer_dif,
    pos_ref, settle_ref, noise_ref, cell_ref, code_ref, table_ref, out_ref, tables, rows_ref, sems,
):
    arch = lax.axis_index("arch")
    tables[0, arch] = table_ref[...]
    fill_table(tables.at[0, 1 - arch], peer_vel, peer_dif, 0)
    sub = sublane()
    fall = jnp.where(is_z(sub), -3.0 * DT, 0.0)

    def block(place):
        j = source_ref[0, place]
        start = pl.multiple_of(j * WIDTH, WIDTH)
        index = cells_of(cell_ref, 0, start, sub)
        noise = stack_halves(noise_ref, (), start)
        here = stack_halves(pos_ref, (), start)
        speed = halves(settle_ref[pl.ds(2 * j, 1), :], settle_ref[pl.ds(2 * j + 1, 1), :], sub)
        here = here + fall * speed
        here = here + advance(tables, 0, tile_ref[0, 0, j] // TILES, index, noise, sub)
        state = halves(code_ref[pl.ds(2 * j, 1), :], code_ref[pl.ds(2 * j + 1, 1), :], sub)
        return encode(here, state, FIRST_CODE, sub)[0:LINES]

    send_chunks(block, rows_ref, out_ref, sems)


def later_kernel(
    tile_ref, route_ref, own_vel, peer_vel, own_dif, peer_dif, noise_ref, cell_ref,
    second_ref, third_ref, source_ref, tables,
):
    arch = lax.axis_index("arch")
    part = pl.program_id(0)

    @pl.when(part == 0)
    def _():
        invert(route_ref, 1, source_ref)
        for step in (1, 2):
            fill_table(tables.at[step - 1, arch], own_vel, own_dif, step)
            fill_table(tables.at[step - 1, 1 - arch], peer_vel, peer_dif, step)

    sub = sublane()

    def block(j, carry):
        start = pl.multiple_of(j * WIDTH, WIDTH)
        slot = part * SPAN + j
        for step in (1, 2):
            index = cells_of(cell_ref, step, start, sub)
            noise = stack_halves(noise_ref, (step,), start)
            out_ref = second_ref if step == 1 else third_ref
            out_ref[j] = advance(
                tables, step - 1, tile_ref[step, 0, slot] // TILES, index, noise, sub
            )
        return carry

    lax.fori_loop(0, SPAN, block, 0, unroll=LATER_UNROLL)


def relay_kernel(source_ref, in_ref, add_ref, out_ref, rows_ref, sems):
    sub = sublane()

    def block(place):
        j = source_ref[0, place]
        word = load_block(in_ref, j)
        here = decode_position(word, FIRST_CODE, sub) + add_ref[j]
        return encode(here, word, SECOND_CODE, sub)[0:LINES]

    send_chunks(block, rows_ref, out_ref, sems)


def decode(code):
    mass = ((code >> 16) + 32768).astype(jnp.float32) * (1.0 / MASS_SCALE)
    frac = (code & 65535).astype(jnp.float32) * (1.0 / FRAC_SCALE)
    return mass, frac


def split_cells(tile_ref, bed_ref, step, row_ref, column_ref):
    def block(slot, carry):
        tile = tile_ref[step, 0, slot] // TILES
        for half in range(2):
            start = pl.multiple_of(slot * WIDTH + half * 128, 128)
            cell = bed_ref[step : step + 1, pl.ds(start, 128)]
            run = pl.ds(2 * slot + half, 1)
            row_ref[run, :] = ((cell >> 6) + tile * 8).astype(jnp.float32)
            column_ref[run, :] = (cell & 63).astype(jnp.float32)
        return carry

    lax.fori_loop(0, NB, block, 0, unroll=16)


def spread_run(ref, run):
    row = jnp.broadcast_to(ref[pl.ds(run, 1), :], (8, 128))
    return jnp.concatenate([row, row], axis=0).astype(jnp.bfloat16)


def histogram(row_ref, column_ref, dep, high_ref, rest_ref, lay_ref):
    high = dep.astype(jnp.bfloat16).astype(jnp.float32)
    high_ref[...] = high
    rest_ref[...] = dep - high
    places = lax.broadcasted_iota(jnp.int32, (64, 128), 0).astype(jnp.float32).astype(jnp.bfloat16)
    one, zero = jnp.bfloat16(1), jnp.bfloat16(0)

    def group(i, total):
        hits = []
        weights = []
        for k in range(2 * GROUP):
            run = 2 * GROUP * i + k
            mine = spread_run(row_ref, run) == places[0:16]
            parts = [jnp.where(mine, spread_run(ref, run), zero) for ref in (high_ref, rest_ref)]
            weights.append(jnp.concatenate(parts, axis=0))
            column = jnp.concatenate([spread_run(column_ref, run)] * 4, axis=0)
            hits.append(jnp.where(column == places, one, zero))
        weight = jnp.concatenate(weights, axis=1)
        hit = jnp.concatenate(hits, axis=1)
        return total + lax.dot_general(
            weight, hit, (((1,), (1,)), ((), ())), preferred_element_type=jnp.float32
        )

    total = lax.fori_loop(0, NB // GROUP, group, jnp.zeros((32, 64), jnp.float32), unroll=4)
    lay_ref[:, 0:64] = total[0:16] + total[16:32]
    return jnp.concatenate([lay_ref[pl.ds(i, 8, stride=2), 0:64] for i in range(2)], axis=1)


def bed_first_kernel(
    tile_ref, bed_ref, mass_ref, settle_ref, out_ref, row_ref, column_ref, *scratch
):
    split_cells(tile_ref, bed_ref, 0, row_ref, column_ref)
    dep = mass_ref[...] * fraction(settle_ref[...])
    out_ref[...] = histogram(row_ref, column_ref, dep, *scratch)


def bed_second_kernel(
    tile_ref, bed_ref, state_ref, before_ref, out_ref, next_row_ref, next_column_ref,
    row_ref, column_ref, *scratch,
):
    split_cells(tile_ref, bed_ref, 1, row_ref, column_ref)
    split_cells(tile_ref, bed_ref, 2, next_row_ref, next_column_ref)
    mass, frac = decode(state_ref[pl.ds(2, 2 * NB, stride=3), :])
    dep = mass * (1.0 - frac) * frac
    out_ref[...] = before_ref[...] + histogram(row_ref, column_ref, dep, *scratch)


def bed_third_kernel(
    row_ref, column_ref, state_ref, before_ref, own_ref, peer_ref, *scratch
):
    mass, frac = decode(state_ref[pl.ds(2, 2 * NB, stride=3), :])
    dep = mass * (1.0 - frac) * (1.0 - frac) * frac
    total = before_ref[...] + histogram(row_ref, column_ref, dep, *scratch)
    total = total * (BEDC / PARTS)
    first = lax.axis_index("arch") == 0
    own_ref[...] = jnp.where(first, total[0:4], total[4:8])
    peer_ref[...] = jnp.where(first, total[4:8], total[0:4])


def finish_kernel(in_ref, add_ref, out_ref, mass_out, rows_ref, mass_ref, sems):
    sub = sublane()
    mass, frac = decode(in_ref[pl.ds(2, 2 * NB, stride=3), :])
    mass_ref[...] = mass * (1.0 - frac) * (1.0 - frac) * (1.0 - frac)
    copies = [pltpu.make_async_copy(mass_ref, mass_out, sems.at[NB // CHUNK])]
    copies[0].start()
    for part in range(NB // CHUNK):

        def block(k, carry, part=part):
            j = part * CHUNK + k
            start = pl.multiple_of(j * WIDTH, WIDTH)
            here = decode_position(load_block(in_ref, j), SECOND_CODE, sub) + add_ref[j]
            rows_ref[:, pl.ds(start, 128)] = here[0:3]
            rows_ref[:, pl.ds(start + 128, 128)] = here[3:6]
            return carry

        lax.fori_loop(0, CHUNK, block, 0, unroll=CHUNK)
        span = pl.ds(part * CHUNK * WIDTH, CHUNK * WIDTH)
        copies.append(
            pltpu.make_async_copy(rows_ref.at[:, span], out_ref.at[:, span], sems.at[part])
        )
        copies[-1].start()
    for copy in copies:
        copy.wait()


def exchange(outgoing):
    blocks = outgoing.reshape(NB, 1, LINES * 128)
    return lax.all_to_all(blocks, "dom", 0, 0, tiled=True).reshape(LINES * NB, 128)


def body(
    position, particle_mass, settling, walk_noise, velocity, diffusivity,
    block_tile, cell_index, bed_cell, route_code,
):
    slabs = velocity.shape[0]
    swap = [(0, 1), (1, 0)]
    vel = velocity.transpose(1, 2, 0, 3).reshape(3, slabs, CELLS)
    dif = diffusivity.transpose(1, 0, 2).reshape(slabs, CELLS)
    peer_vel = lax.ppermute(vel, "arch", swap)
    peer_dif = lax.ppermute(dif, "arch", swap)
    mass = particle_mass.reshape(2 * NB, 128)
    settle = settling.reshape(2 * NB, 128)

    state_type = jax.ShapeDtypeStruct((LINES * NB, 128), jnp.int32)
    move_type = jax.ShapeDtypeStruct((NB, 8, 128), jnp.float32)
    bed_type = jax.ShapeDtypeStruct((8, 128), jnp.float32)
    steps = NB // SPAN
    span = SPAN * WIDTH
    runs = jax.ShapeDtypeStruct((2 * NB, 128), jnp.float32)
    bed_scratch = [in_vmem(runs), in_vmem(runs), pltpu.VMEM((16, 128), jnp.float32)]

    *loaded, tiles, sources = pl.pallas_call(
        load_kernel,
        in_specs=[whole(pl.ANY)] * 9,
        out_specs=[whole()] * 6 + [whole(SMEM)] * 2,
        out_shape=[
            pltpu.VMEM((3, PARTS), jnp.float32),
            in_vmem(runs),
            pltpu.VMEM((3, PARTS), jnp.float32),
            pltpu.VMEM((3, PARTS), jnp.int32),
            pltpu.VMEM((2 * NB, 128), jnp.int32),
            pltpu.VMEM((ROWS, 8, 128), jnp.float32),
            pltpu.SMEM(block_tile.shape, jnp.int32),
            pltpu.SMEM((1, NB), jnp.int32),
        ],
        scratch_shapes=[
            in_vmem(runs), in_vmem(vel), in_vmem(dif),
            pltpu.SMEM(route_code.shape, jnp.int32), pltpu.SemaphoreType.DMA((9,)),
        ],
        compiler_params=params(),
        cost_estimate=pl.CostEstimate(flops=10**7, bytes_accessed=4 * 10**6, transcendentals=0),
        name="load",
    )(
        *in_hbm(route_code, block_tile, vel, dif),
        *in_hbm(position, mass, settle, walk_noise, cell_index),
    )

    send_scratch = [
        pltpu.VMEM((LINES * NB, 128), jnp.int32), pltpu.SemaphoreType.DMA((NB // CHUNK,)),
    ]
    outgoing = pl.pallas_call(
        first_kernel,
        in_specs=[whole(SMEM), whole(SMEM)] + [whole()] * 8,
        out_specs=whole(pltpu.HBM),
        out_shape=state_type,
        scratch_shapes=[pltpu.VMEM((1, 2, ROWS, 8, 128), jnp.float32)] + send_scratch,
        compiler_params=params(),
        name="first",
    )(tiles, sources, peer_vel, peer_dif, *loaded)

    incoming = exchange(outgoing)

    second, third, later_sources = pl.pallas_call(
        later_kernel,
        grid=(steps,),
        in_specs=[whole(SMEM), whole(SMEM), whole(), whole(), whole(), whole()]
        + [
            pl.BlockSpec((3, 3, span), lambda i: (0, 0, i)),
            pl.BlockSpec((3, span), lambda i: (0, i)),
        ],
        out_specs=[pl.BlockSpec((SPAN, 8, 128), lambda i: (i, 0, 0))] * 2 + [whole(SMEM)],
        out_shape=[in_vmem(move_type), in_vmem(move_type), pltpu.SMEM((1, NB), jnp.int32)],
        scratch_shapes=[pltpu.VMEM((2, 2, ROWS, 8, 128), jnp.float32)],
        compiler_params=params(),
        cost_estimate=pl.CostEstimate(flops=10**9, bytes_accessed=10**7, transcendentals=0),
        name="later",
    )(*in_hbm(block_tile, route_code, vel), peer_vel, *in_hbm(dif), peer_dif, *in_hbm(walk_noise, cell_index))

    bed = pl.pallas_call(
        bed_first_kernel,
        in_specs=[whole(SMEM), whole(), whole(), whole()],
        out_specs=whole(),
        out_shape=bed_type,
        scratch_shapes=[in_vmem(runs), in_vmem(runs)] + bed_scratch,
        compiler_params=params(),
        cost_estimate=pl.CostEstimate(flops=10**9, bytes_accessed=10**7, transcendentals=0),
        name="bed_first",
    )(block_tile, bed_cell, mass, settle)

    outgoing = pl.pallas_call(
        relay_kernel,
        in_specs=[whole(SMEM), whole(), whole()],
        out_specs=whole(pltpu.HBM),
        out_shape=state_type,
        scratch_shapes=send_scratch,
        compiler_params=params(),
        name="relay",
    )(later_sources, incoming, second)

    bed, row, column = pl.pallas_call(
        bed_second_kernel,
        in_specs=[whole(SMEM), whole(), whole(), whole()],
        out_specs=[whole(), whole(), whole()],
        out_shape=[bed_type, in_vmem(runs), in_vmem(runs)],
        scratch_shapes=[in_vmem(runs), in_vmem(runs)] + bed_scratch,
        compiler_params=params(),
        cost_estimate=pl.CostEstimate(flops=10**9, bytes_accessed=10**7, transcendentals=0),
        name="bed_second",
    )(block_tile, bed_cell, incoming, bed)

    incoming = exchange(outgoing)

    own, peer = pl.pallas_call(
        bed_third_kernel,
        in_specs=[whole()] * 4,
        out_specs=[whole(), whole()],
        out_shape=[
            jax.ShapeDtypeStruct((4, 128), jnp.float32),
            jax.ShapeDtypeStruct((4, 128), jnp.float32),
        ],
        scratch_shapes=bed_scratch,
        compiler_params=params(),
        name="bed_third",
    )(row, column, incoming, bed)
    other = lax.ppermute(peer, "arch", swap)

    final_position, final_mass = pl.pallas_call(
        finish_kernel,
        in_specs=[whole(), whole()],
        out_specs=[whole(pltpu.HBM), whole(pltpu.HBM)],
        out_shape=[jax.ShapeDtypeStruct((3, PARTS), jnp.float32), runs],
        scratch_shapes=[
            pltpu.VMEM((3, PARTS), jnp.float32), in_vmem(runs),
            pltpu.SemaphoreType.DMA((NB // CHUNK + 1,)),
        ],
        compiler_params=params(),
        cost_estimate=pl.CostEstimate(flops=10**7, bytes_accessed=10**6, transcendentals=0),
        name="finish",
    )(incoming, third)
    return (
        final_position,
        final_mass.reshape(PARTS),
        (own + other).reshape(1, BEDC),
    )


def solution(mesh):
    one = P(("arch", "dom"))
    two = P(None, ("arch", "dom"))
    rows = P(None, ("arch", "dom"), None)
    return jax.shard_map(
        body,
        mesh=mesh,
        in_specs=(
            two, one, one, P(None, None, ("arch", "dom")),
            P(None, None, ("arch", "dom"), None), rows, rows, two, two, rows,
        ),
        out_specs=(two, one, P(("arch", "dom"), None)),
        check_vma=False,
    )
```
